128 devices in a mesh: tm: 16 (over y_lo, x, core), height: 8 (over z, y_hi).
Axes of the slice: x: 4, y: 4 (y_hi: 2, y_lo: 2; y = y_hi * 2 + y_lo), z: 4, core: 2. Of those that a mesh axis runs over, the one named last changes fastest.
Arguments:
- query_band: bfloat16 [48, 24, 24, 2048], P('tm', 'height'), may hold values from -4.5 to 4.5
- key_band: bfloat16 [48, 24, 24, 2048], P('tm', 'height'), may hold values from -11 to 11
- value_band: bfloat16 [48, 24, 24, 2048], P('tm', 'height'), may hold values from -6 to 6
Outputs:
- attended: bfloat16 [48, 24, 24, 2048], P('tm', 'height')
The draws below stay inside these ranges and needn't reach their ends.
All inputs are finite; a program needn't handle non-finite values.
Results may differ from the reference program's by a relative error of at most 0.0033.
Values may be sent and summed in bfloat16 or wider, within the bound.
No kernel may reach another device: no remote copies, remote signals or barrier semaphores. Data moves between devices by JAX's collectives and lax.ppermute only.
A program may use at most 128 MiB of HBM per device.

```python
import jax
import jax.numpy as jnp
from jax import lax

HEADS = 16
HEAD_DIM = 128
TILE_T = 6
TILE_H = 8
TILE_W = 8
FEAT = 2048
FRAMES = 48
ROWS = 24
COLS = 24


def draw_query_band(key, part):
    key = jax.random.fold_in(key, 1)
    grid_shape = (FRAMES, ROWS, COLS, HEADS * HEAD_DIM)
    drawn = jnp.clip(jax.random.normal(key, grid_shape, jnp.float32), -4.5, 4.5)
    return drawn.astype(jnp.bfloat16)


def draw_key_band(key, part):
    key = jax.random.fold_in(key, 2)
    grid_shape = (FRAMES, ROWS, COLS, HEADS * HEAD_DIM)
    drawn = jnp.clip(2.5 * jax.random.normal(key, grid_shape, jnp.float32), -11.0, 11.0)
    return drawn.astype(jnp.bfloat16)


def level_of(key, dims, shards, low, top_value):
    level = 1.0
    for position, blocks in shards:
        steps = jax.random.uniform(jax.random.fold_in(jax.random.fold_in(key, 6), position), (blocks,), jnp.float32, low / len(shards), top_value / len(shards))
        level = level * jnp.repeat(jnp.exp(steps), dims[position] // blocks).reshape((-1,) + (1,) * (len(dims) - 1 - position))
    return level


def noise(key, extent, scale, most, cuts=(), kind=jnp.bfloat16):
    level = level_of(key, extent, cuts, -0.22, 0.18) if cuts else 1.0
    values = jax.random.normal(key, extent, jnp.float32) * scale * level
    return jnp.minimum(jnp.maximum(values, -most), most).astype(kind)


def setup_inputs(seed: int = 0) -> dict:
    seeds = jax.random.split(jax.random.key(seed), 4)
    query_band = draw_query_band(jax.random.fold_in(seeds[3], 71), 0)
    key_band = draw_key_band(jax.random.fold_in(seeds[3], 71), 0)
    value_band = noise(seeds[2], (FRAMES, ROWS, COLS, FEAT), 1.0, 6.0, ((0, 16), (1, 8)))
    return dict(query_band=query_band, key_band=key_band, value_band=value_band)


def attend_tile(queries, key_rows, value_rows, usable):
    def one_head(head_index):
        first_column = head_index * HEAD_DIM
        query_part = lax.dynamic_slice_in_dim(queries, first_column, HEAD_DIM, 1)
        key_part = lax.dynamic_slice_in_dim(key_rows, first_column, HEAD_DIM, 1)
        value_part = lax.dynamic_slice_in_dim(value_rows, first_column, HEAD_DIM, 1)
        scores = lax.dot_general(query_part, key_part, (((1,), (1,)), ((), ())), preferred_element_type=jnp.float32) * (HEAD_DIM ** -0.5)
        scores = jnp.where(usable[None, :], scores, jnp.float32(-1e30))
        largest = jnp.max(scores, axis=1, keepdims=True)
        weights = lax.optimization_barrier(jnp.exp(scores - largest).astype(jnp.bfloat16))
        weight_sum = jnp.sum(weights.astype(jnp.float32), axis=1, keepdims=True)
        return jnp.dot(weights, value_part, preferred_element_type=jnp.float32) / weight_sum

    stacked = lax.map(one_head, jnp.arange(HEADS, dtype=jnp.int32))
    return jnp.transpose(stacked, (1, 0, 2)).reshape(queries.shape[0], HEADS * HEAD_DIM).astype(jnp.bfloat16)


def reference(query_band, key_band, value_band):
    time_tiles = FRAMES // TILE_T
    row_tiles = ROWS // TILE_H
    col_tiles = COLS // TILE_W
    feature_count = HEADS * HEAD_DIM
    zero_index = jnp.zeros((), jnp.int32)
    frame_local = jnp.arange(3 * TILE_T, dtype=jnp.int32) // TILE_T
    row_local = jnp.arange(3 * TILE_H, dtype=jnp.int32) // TILE_H
    col_local = jnp.arange(3 * TILE_W, dtype=jnp.int32) // TILE_W
    grid_shape = (3 * TILE_T, 3 * TILE_H, 3 * TILE_W)

    def one_tile(tile_id):
        time_index = (tile_id // (row_tiles * col_tiles)).astype(jnp.int32)
        row_index = ((tile_id // col_tiles) % row_tiles).astype(jnp.int32)
        col_index = (tile_id % col_tiles).astype(jnp.int32)
        start_time = jnp.clip(time_index - 1, 0, time_tiles - 3).astype(jnp.int32)
        start_row = jnp.clip(row_index - 1, 0, row_tiles - 3).astype(jnp.int32)
        start_col = jnp.clip(col_index - 1, 0, col_tiles - 3).astype(jnp.int32)
        tile_queries = lax.dynamic_slice(query_band, (time_index * TILE_T, row_index * TILE_H, col_index * TILE_W, zero_index), (TILE_T, TILE_H, TILE_W, feature_count)).reshape(-1, feature_count)
        corner = (start_time * TILE_T, start_row * TILE_H, start_col * TILE_W, zero_index)
        key_rows = lax.dynamic_slice(key_band, corner, (3 * TILE_T, 3 * TILE_H, 3 * TILE_W, feature_count)).reshape(-1, feature_count)
        value_rows = lax.dynamic_slice(value_band, corner, (3 * TILE_T, 3 * TILE_H, 3 * TILE_W, feature_count)).reshape(-1, feature_count)
        time_near = jnp.abs(start_time + frame_local - time_index) <= 1
        row_near = jnp.abs(start_row + row_local - row_index) <= 1
        col_near = jnp.abs(start_col + col_local - col_index) <= 1
        usable = jnp.broadcast_to(time_near[:, None, None] & row_near[None, :, None] & col_near[None, None, :], grid_shape).reshape(-1)
        return attend_tile(tile_queries, key_rows, value_rows, usable)

    results = lax.map(one_tile, jnp.arange(time_tiles * row_tiles * col_tiles, dtype=jnp.int32))
    results = results.reshape(time_tiles, row_tiles, col_tiles, TILE_T, TILE_H, TILE_W, feature_count)
    return jnp.transpose(results, (0, 3, 1, 4, 2, 5, 6)).reshape(FRAMES, ROWS, COLS, feature_count)
```

```python
import functools

import jax
import jax.numpy as jnp
from jax import lax
from jax.experimental import pallas as pl
from jax.experimental.pallas import tpu as pltpu
from jax.sharding import Mesh, PartitionSpec as P

HEAD_DIM = 128
HEADS = 16
BLOCK = 384
HALF = 192
LOG2E = 1.4426950408889634
SCORE_SCALE = HEAD_DIM ** (-0.5) * LOG2E
LOWEST = -1e30
VMEM = 56 * 1024 * 1024
PARAMS = dict(vmem_limit_bytes=VMEM)

CHUNK = (9, 24, HEAD_DIM)


def pack_kernel(core_ref, x_ref, o_ref):
    for h in range(4):
        part = x_ref[:, :, :, h * HEAD_DIM : (h + 1) * HEAD_DIM].astype(jnp.float32)
        for c in range(3):
            for r in range(3):
                piece = jnp.concatenate([part[f, r, c * 8 : (c + 1) * 8] for f in range(3)], axis=0)
                o_ref[h, c * 3 + r] = piece.astype(jnp.bfloat16)


def pack(core, x):
    return pl.pallas_call(
        pack_kernel,
        grid_spec=pltpu.PrefetchScalarGridSpec(
            num_scalar_prefetch=1,
            grid=(4,),
            in_specs=[pl.BlockSpec((3, 3, 24, 512), lambda j, s: (0, 0, 0, (j + 2 * s[0]) % 4))],
            out_specs=pl.BlockSpec((4,) + CHUNK, lambda j, s: (j, 0, 0, 0)),
        ),
        out_shape=jax.ShapeDtypeStruct((HEADS,) + CHUNK, jnp.bfloat16),
        compiler_params=pltpu.CompilerParams(**PARAMS),
        name="pack",
    )(core, x)


def unpack_kernel(core_ref, x_ref, o_ref):
    for h in range(4):
        for r in range(3):
            parts = [x_ref[h, c * 3 + r].astype(jnp.float32) for c in range(3)]
            for f in range(3):
                piece = jnp.concatenate([p[f * 8 : (f + 1) * 8] for p in parts], axis=0)
                o_ref[f, r, :, h * HEAD_DIM : (h + 1) * HEAD_DIM] = piece.astype(jnp.bfloat16)


def unpack(core, x):
    return pl.pallas_call(
        unpack_kernel,
        grid_spec=pltpu.PrefetchScalarGridSpec(
            num_scalar_prefetch=1,
            grid=(4,),
            in_specs=[pl.BlockSpec((4,) + CHUNK, lambda j, s: (j, 0, 0, 0))],
            out_specs=pl.BlockSpec((3, 3, 24, 512), lambda j, s: (0, 0, 0, (j + 2 * s[0]) % 4)),
        ),
        out_shape=jax.ShapeDtypeStruct((3, 3, 24, HEADS * HEAD_DIM), jnp.bfloat16),
        compiler_params=pltpu.CompilerParams(**PARAMS),
        name="unpack",
    )(core, x)


def assemble_kernel(kept_ref, came_ref, o_ref):
    for b in range(3):
        halves = []
        for ref in (kept_ref, came_ref):
            for row in range(8 * b, 8 * b + 8):
                halves.append(ref[row // 3, row % 3].astype(jnp.float32))
        o_ref[0, b] = jnp.concatenate(halves, axis=0).astype(jnp.bfloat16)


def assemble(kept, came):
    spec = pl.BlockSpec((8, 3, 24, HEAD_DIM), lambda c: (0, c, 0, 0))
    return pl.pallas_call(
        assemble_kernel,
        grid=(3,),
        in_specs=[spec, spec],
        out_specs=pl.BlockSpec((1, 3, BLOCK, HEAD_DIM), lambda c: (c, 0, 0, 0)),
        out_shape=jax.ShapeDtypeStruct((3, 3, BLOCK, HEAD_DIM), jnp.bfloat16),
        compiler_params=pltpu.CompilerParams(**PARAMS),
        name="assemble",
    )(kept, came)


SUB = 128


def attend_kernel(sides, first, last, q_low, p_low, p_high, v_low, *refs):
    refs = list(refs)
    flag_ref = refs.pop(0)
    q_ref = refs.pop(0)
    pairs = [(refs.pop(0), refs.pop(0)) for _ in range(sides)]
    if not first:
        acc_in, top_in = refs.pop(0), refs.pop(0)
    if last:
        kept_ref, sent_ref = refs.pop(0), refs.pop(0)
    else:
        acc_out, top_out = refs.pop(0), refs.pop(0)
    acc_ref, top_ref = refs
    step_id = pl.program_id(0)
    col = step_id // 3 + q_low
    band = step_id % 3
    if first:
        acc_ref[...] = jnp.zeros_like(acc_ref)
        top_ref[...] = jnp.full_like(top_ref, LOWEST)
    else:
        acc_ref[...] = acc_in[0]
        top_ref[...] = top_in[0]
    lowest = jnp.maximum(col - 1, p_low)
    highest = jnp.minimum(col + 1, p_high)
    for side in range(sides):
        k_ref, v_ref = pairs[side]

        def chunk(p, bands, start, k_ref=k_ref, v_ref=v_ref):
            keys = k_ref[p, pl.ds(start, bands)].reshape(bands * BLOCK, HEAD_DIM)
            values = v_ref[p - v_low, pl.ds(start, bands)].reshape(bands * BLOCK, HEAD_DIM)
            values = jnp.concatenate([values, jnp.ones_like(values)], axis=1)
            for s in range(BLOCK // SUB):
                rows = pl.ds(s * SUB, SUB)
                scores = lax.dot_general(
                    q_ref[0, 0, rows], keys, (((1,), (1,)), ((), ())), preferred_element_type=jnp.float32
                )
                before = top_ref[rows, :1]
                top = jnp.maximum(before, jnp.max(scores, axis=1, keepdims=True) * SCORE_SCALE)
                weights = jnp.exp2(scores * SCORE_SCALE - top).astype(jnp.bfloat16)
                fade = jnp.exp2(before - top)
                acc_ref[rows, :] = acc_ref[rows, :] * fade + jnp.dot(
                    weights, values, preferred_element_type=jnp.float32
                )
                top_ref[rows, :] = jnp.broadcast_to(top, (SUB, HEAD_DIM))

        def one(p, carry, chunk=chunk):
            @pl.when(band == 1)
            def _():
                chunk(p, 3, 0)

            @pl.when(band != 1)
            def _():
                chunk(p, 2, band // 2)

            return carry

        if sides == 1:
            lax.fori_loop(lowest, highest + 1, one, 0)
        else:

            @pl.when(flag_ref[side] != 0)
            def _(one=one):
                lax.fori_loop(lowest, highest + 1, one, 0)

    if not last:
        acc_out[0] = acc_ref[...]
        top_out[0] = top_ref[...]
        return
    result = acc_ref[:, :HEAD_DIM] / acc_ref[:, HEAD_DIM:]
    for b in range(3):

        @pl.when(band == b)
        def _(b=b):
            for half, ref in enumerate((kept_ref, sent_ref)):
                for n in range(8):
                    row = 8 * b + n
                    at = half * HALF + n * 24
                    ref[row // 3, row % 3] = result[at : at + 24].astype(jnp.bfloat16)


def attend(flags, q, pairs, state=None, last=False, cols=(0, 2), part=(0, 2), v_low=0):
    first = state is None
    q_low = cols[0]
    steps = 3 * (cols[1] - cols[0] + 1)
    tile = lambda i, s: (i // 3 + q_low, i % 3, 0, 0)
    flat = lambda i, s: (i + 3 * q_low, 0, 0)
    in_specs = [pl.BlockSpec((1, 1, BLOCK, HEAD_DIM), tile)]
    operands = [q]
    for k, v in pairs:
        for a in (k, v):
            in_specs.append(pl.BlockSpec(a.shape, lambda i, s: (0, 0, 0, 0)))
            operands.append(a)
    acc_spec = pl.BlockSpec((1, BLOCK, 2 * HEAD_DIM), flat)
    top_spec = pl.BlockSpec((1, BLOCK, HEAD_DIM), flat)
    state_shape = [
        jax.ShapeDtypeStruct((9, BLOCK, 2 * HEAD_DIM), jnp.float32),
        jax.ShapeDtypeStruct((9, BLOCK, HEAD_DIM), jnp.float32),
    ]
    if not first:
        in_specs += [acc_spec, top_spec]
        operands += list(state)
    if last:
        out_specs = [pl.BlockSpec((8, 3, 24, HEAD_DIM), lambda i, s: (0, i // 3, 0, 0))] * 2
        out_shape = [jax.ShapeDtypeStruct((8, 3 * (cols[1] - cols[0] + 1), 24, HEAD_DIM), jnp.bfloat16)] * 2
    else:
        out_specs = [acc_spec, top_spec]
        out_shape = state_shape
    kernel = functools.partial(attend_kernel, len(pairs), first, last, q_low, part[0], part[1], v_low)
    return pl.pallas_call(
        kernel,
        grid_spec=pltpu.PrefetchScalarGridSpec(
            num_scalar_prefetch=1,
            grid=(steps,),
            in_specs=in_specs,
            out_specs=out_specs,
            scratch_shapes=[
                pltpu.VMEM((BLOCK, 2 * HEAD_DIM), jnp.float32),
                pltpu.VMEM((BLOCK, HEAD_DIM), jnp.float32),
            ],
        ),
        out_shape=out_shape,
        compiler_params=pltpu.CompilerParams(**PARAMS),
        name="attend",
    )(flags, *operands)


PLANE = ("ylo", "core", "z", "yhi")


def plane_groups():
    at = lambda ylo, core, n: (ylo * 2 + core) * 8 + n
    first = [at(ylo, 0, n) for ylo in (0, 1) for n in range(8)]
    second = [at(ylo, 1, n) for ylo in (1, 0) for n in range(8)]
    return [first, second]


def exchange(x):
    return lax.all_to_all(x, PLANE, 0, 0, axis_index_groups=plane_groups(), tiled=True)


def swap_cores(x):
    return lax.ppermute(x, "core", [(0, 1), (1, 0)])


def from_tile(x, steps):
    at = lambda tile: (tile % 4) * 2 + tile // 4
    return lax.ppermute(
        x, ("x", "core"), [(at(t), at(t + steps)) for t in range(8) if 0 <= t + steps < 8]
    )


def body(query_band, key_band, value_band):
    core_index = lax.axis_index("core").astype(jnp.int32)
    core = core_index.reshape(1)
    tile = core_index * 4 + lax.axis_index("x").astype(jnp.int32)
    flags = jnp.stack([tile > 0, tile < 7]).astype(jnp.int32)

    def to_tile(band):
        got = exchange(pack(core, band))
        return assemble(got, swap_cores(got[8:]))

    keys = to_tile(key_band)
    keys_near = [from_tile(keys, s) for s in (1, -1)]
    queries = to_tile(query_band)
    values = to_tile(value_band)
    values_near = [from_tile(values, s) for s in (1, -1)]
    state = attend(flags, queries, [(keys, values)])
    kept, sent = attend(flags, queries, list(zip(keys_near, values_near)), state, last=True)
    back = jnp.concatenate([kept, swap_cores(sent)], axis=0)
    return unpack(core, exchange(back))


def solution(mesh):
    split = Mesh(mesh.devices.reshape(2, 4, 2, 4, 2), ("ylo", "x", "core", "z", "yhi"))
    spec = P(("ylo", "x", "core"), ("z", "yhi"), None, None)
    return jax.shard_map(body, mesh=split, in_specs=(spec, spec, spec), out_specs=spec, check_vma=False)
```

```python
import functools

import jax
import jax.numpy as jnp
from jax import lax
from jax.experimental import pallas as pl
from jax.experimental.pallas import tpu as pltpu
from jax.sharding import Mesh, PartitionSpec as P

HEAD_DIM = 128
HEADS = 16
BLOCK = 384
HALF = 192
SCORE_SCALE = HEAD_DIM ** (-0.5) * 1.4426950408889634
LOWEST = -1e30
OVER = 2.0**100
BF16 = jnp.bfloat16
F32 = jnp.float32
CHUNK = (9, 24, HEAD_DIM)
NT = (((1,), (1,)), ((), ()))
TN = (((0,), (0,)), ((), ()))


def params():
    return pltpu.CompilerParams(vmem_limit_bytes=56 * 1024 * 1024)


def cost(us):
    return pl.CostEstimate(flops=int(us * 1e-6 * 1.1e15), bytes_accessed=int(us * 1e-6 * 3.3e12), transcendentals=0)


def pack_kernel(*refs):
    o_ref = refs[-1]
    for n, x_ref in enumerate(refs[:-1]):
        for h in range(8):
            o_ref[h, n] = x_ref[:, :, :, h * HEAD_DIM : (h + 1) * HEAD_DIM].reshape(CHUNK)


def pack(*bands):
    count = len(bands)
    return pl.pallas_call(
        pack_kernel,
        grid=(2,),
        in_specs=[pl.BlockSpec((3, 3, 24, 1024), lambda j: (0, 0, 0, j))] * count,
        out_specs=pl.BlockSpec((8, count) + CHUNK, lambda j: (j, 0, 0, 0, 0)),
        out_shape=jax.ShapeDtypeStruct((HEADS, count) + CHUNK, BF16),
        compiler_params=params(),
        cost_estimate=cost(2 * count),
        name="pack",
    )(*bands)


def unpack_kernel(x_ref, o_ref):
    for h in range(8):
        o_ref[:, :, :, h * HEAD_DIM : (h + 1) * HEAD_DIM] = x_ref[h].reshape(3, 3, 24, HEAD_DIM)


def unpack(x):
    return pl.pallas_call(
        unpack_kernel,
        grid=(2,),
        in_specs=[pl.BlockSpec((8,) + CHUNK, lambda j: (j, 0, 0, 0))],
        out_specs=pl.BlockSpec((3, 3, 24, 1024), lambda j: (0, 0, 0, j)),
        out_shape=jax.ShapeDtypeStruct((3, 3, 24, HEADS * HEAD_DIM), BF16),
        compiler_params=params(),
        cost_estimate=cost(2),
        name="unpack",
    )(x)


def assemble_kernel(cuts, got_ref, *o_refs):
    for b in range(3):
        n = [b in cut for cut in cuts].index(True)
        for m in range(got_ref.shape[1]):
            for half in range(2):
                slabs = [
                    got_ref[half * 8 + row // 3, m, f * 3 + row % 3].astype(F32)
                    for f in range(3)
                    for row in range(8 * b, 8 * b + 8)
                ]
                for c in range(3):
                    tokens = jnp.concatenate([s[c * 8 : (c + 1) * 8] for s in slabs], axis=0)
                    o_refs[n][m, b - cuts[n][0], c, half * HALF : (half + 1) * HALF] = tokens.astype(BF16)


def assemble(got, first, count, cuts):
    shapes = [(count, len(cut), 3, BLOCK, HEAD_DIM) for cut in cuts]
    whole = lambda shape: pl.BlockSpec(shape, lambda i, n=len(shape): (0,) * n)
    return pl.pallas_call(
        functools.partial(assemble_kernel, cuts),
        grid=(1,),
        in_specs=[pl.BlockSpec((16, count) + CHUNK, lambda i: (0, first // count, 0, 0, 0))],
        out_specs=[whole(s) for s in shapes],
        out_shape=[jax.ShapeDtypeStruct(s, BF16) for s in shapes],
        compiler_params=params(),
        cost_estimate=cost(2 * count),
        name="assemble",
    )(got)


def near(n):
    return range(max(n - 1, 0), min(n + 1, 2) + 1)


def attend_kernel(plan, *refs):
    own, last, cuts, q_bands = plan
    refs = list(refs)
    sides = 1 if own else 2
    flag_ref = None if own else refs.pop(0)
    q_ref = refs.pop(0)
    kv = [{}, {}]
    for side in range(sides):
        for cut in cuts:
            ref = refs.pop(0)
            for p in cut:
                kv[side][p] = (ref, p - cut[0])
    k_bands = [p for cut in cuts for p in cut]
    if not own:
        acc_in, row_in = refs.pop(0), refs.pop(0)
    if last:
        o_ref = refs.pop(0)
    acc_out, row_out = refs

    def tile(which, side, p, c):
        ref, at = kv[side][p]
        return ref[which, at, c]

    def run(which, places, cols):
        wide = len(cols) * BLOCK
        parts = []
        for p, side in places:
            ref, at = kv[side][p]
            parts.append(ref[which, at, cols[0] : cols[-1] + 1].reshape(wide, HEAD_DIM))
        return jnp.concatenate(parts, axis=0)

    worst = jnp.zeros((1, BLOCK), F32)
    for b in range(3):
        for c in range(3):
            at = 3 * b + c
            if b not in q_bands:
                acc_out[at] = acc_in[at]
                row_out[at] = row_in[at]
                continue
            q = q_ref[0, b, c]
            places = [(p, side) for p in k_bands if p in near(b) for side in range(sides)]
            cols = list(near(c))
            wide = len(cols) * BLOCK
            scores = lax.dot_general(run(0, places, cols), q, NT, preferred_element_type=F32)
            if own:
                mine = (places.index((b, 0)) * len(cols) + cols.index(c)) * BLOCK
                top = jnp.max(scores[mine : mine + BLOCK], axis=0, keepdims=True) * SCORE_SCALE
                tops = [top]
            else:
                top = row_in[at, 1:2]
                tops = [top + (1 - flag_ref[side]).astype(F32) * 1e30 for side in range(sides)]
            weights = jnp.concatenate(
                [
                    jnp.exp2(scores[n * wide : (n + 1) * wide] * SCORE_SCALE - tops[side])
                    for n, (p, side) in enumerate(places)
                ],
                axis=0,
            )
            total = jnp.sum(weights, axis=0, keepdims=True)
            acc = lax.dot_general(run(1, places, cols), weights.astype(BF16), TN, preferred_element_type=F32)
            if not own:
                acc = acc + acc_in[at]
                total = total + row_in[at, 0:1]
            acc_out[at] = acc
            row_out[at] = jnp.concatenate([total, top, jnp.zeros((6, BLOCK), F32)], axis=0)
            worst = jnp.maximum(worst, jnp.where(total < OVER, 0.0, 1.0))

    @pl.when(jnp.max(worst) > 0.0)
    def _():
        for b in q_bands:

            def redo(c, carry, b=b):
                at = 3 * b + c
                q = q_ref[0, b, c]
                if own:
                    acc_out[at] = jnp.zeros((HEAD_DIM, BLOCK), F32)
                    row_out[at, 0:1] = jnp.zeros((1, BLOCK), F32)
                    row_out[at, 1:2] = jnp.full((1, BLOCK), LOWEST, F32)
                else:
                    acc_out[at] = acc_in[at]
                    row_out[at] = row_in[at]
                for side in range(sides):
                    for p in k_bands:
                        if p not in near(b):
                            continue

                        def some(k, carry, side=side, p=p):
                            scores = lax.dot_general(tile(0, side, p, k), q, NT, preferred_element_type=F32)
                            before = row_out[at, 1:2]
                            top = jnp.maximum(before, jnp.max(scores, axis=0, keepdims=True) * SCORE_SCALE)
                            weights = jnp.exp2(scores * SCORE_SCALE - top)
                            fade = jnp.exp2(before - top)
                            acc = lax.dot_general(
                                tile(1, side, p, k), weights.astype(BF16), TN, preferred_element_type=F32
                            )
                            acc_out[at] = acc_out[at] * fade + acc
                            row_out[at, 0:1] = row_out[at, 0:1] * fade + jnp.sum(weights, axis=0, keepdims=True)
                            row_out[at, 1:2] = top
                            return carry

                        low, high = jnp.maximum(c - 1, 0), jnp.minimum(c + 1, 2) + 1
                        if own:
                            lax.fori_loop(low, high, some, 0)
                        else:

                            @pl.when(flag_ref[side] != 0)
                            def _(some=some, low=low, high=high):
                                lax.fori_loop(low, high, some, 0)

                return carry

            lax.fori_loop(0, 3, redo, 0)

    if last:
        for b in range(3):
            tiles = [(acc_out[3 * b + c] / row_out[3 * b + c, 0:1]).T for c in range(3)]
            for half in range(2):
                for f in range(3):
                    for n in range(8):
                        row = 8 * b + n
                        at = half * HALF + f * 64 + n * 8
                        slab = jnp.concatenate([t[at : at + 8] for t in tiles], axis=0)
                        o_ref[half * 8 + row // 3, f * 3 + row % 3] = slab.astype(BF16)


ACC = (9, HEAD_DIM, BLOCK)
ROW = (9, 8, BLOCK)


def attend(queries, keys_values, cuts, flags=None, state=None, last=False, us=12):
    own = state is None
    k_bands = [p for cut in cuts for p in cut]
    q_bands = [b for b in range(3) if any(p in near(b) for p in k_bands)]
    operands = [queries] + [a for side in keys_values for a in side]
    in_specs = []
    if not own:
        operands = [flags] + operands + list(state)
        in_specs.append(pl.BlockSpec(memory_space=pltpu.SMEM))
    in_specs += [pl.BlockSpec(memory_space=pltpu.VMEM)] * (len(operands) - len(in_specs))
    state_shapes = [jax.ShapeDtypeStruct(ACC, F32), jax.ShapeDtypeStruct(ROW, F32)]
    if last:
        out_shape = [jax.ShapeDtypeStruct((16,) + CHUNK, BF16)]
        scratch = [pltpu.VMEM(s.shape, F32) for s in state_shapes]
    else:
        out_shape, scratch = state_shapes, []
    return pl.pallas_call(
        functools.partial(attend_kernel, (own, last, cuts, q_bands)),
        in_specs=in_specs,
        out_specs=[pl.BlockSpec(memory_space=pltpu.VMEM)] * len(out_shape),
        out_shape=out_shape,
        scratch_shapes=scratch,
        compiler_params=params(),
        cost_estimate=cost(us),
        name="attend",
    )(*operands)


PLANE = ("core", "z", "yhi")


def exchange(x):
    return lax.all_to_all(x, PLANE, 0, 0, tiled=True)


def from_tile(x, steps):
    return lax.ppermute(x, ("ylo", "x"), [(t, t + steps) for t in range(8) if 0 <= t + steps < 8])


CUTS = ((0, 1), (2,))


def body(query_band, key_band, value_band):
    tile = (lax.axis_index("ylo") * 4 + lax.axis_index("x")).astype(jnp.int32)
    flags = jnp.stack([tile > 0, tile < 7]).astype(jnp.int32)
    got = exchange(pack(key_band, value_band, query_band))
    here = assemble(got, 0, 2, CUTS)
    near_tiles = [[from_tile(a, s) for s in (1, -1)] for a in here]
    (queries,) = assemble(got, 2, 1, ((0, 1, 2),))
    state = attend(queries, [here], CUTS, us=12)
    for n, cut in enumerate(CUTS):
        state = attend(
            queries, [[a] for a in near_tiles[n]], (cut,), flags, state, last=n == len(CUTS) - 1, us=9 * len(cut)
        )
    return unpack(exchange(state[0]))


def solution(mesh):
    split = Mesh(mesh.devices.reshape(2, 4, 2, 4, 2), ("ylo", "x", "core", "z", "yhi"))
    spec = P(("ylo", "x", "core"), ("z", "yhi"), None, None)
    return jax.shard_map(body, mesh=split, in_specs=(spec, spec, spec), out_specs=spec, check_vma=False)
```

```python
import functools

import jax
import jax.numpy as jnp
from jax import lax
from jax.experimental import pallas as pl
from jax.experimental.pallas import tpu as pltpu
from jax.sharding import Mesh, PartitionSpec as P

HEAD_DIM = 128
HEADS = 16
BLOCK = 384
HALF = 192
SCORE_SCALE = HEAD_DIM ** (-0.5) * 1.4426950408889634
LOWEST = -1e30
OVER = 2.0**100
BF16 = jnp.bfloat16
F32 = jnp.float32
CHUNK = (9, 24, HEAD_DIM)
NT = (((1,), (1,)), ((), ()))
TN = (((0,), (0,)), ((), ()))


def params():
    return pltpu.CompilerParams(vmem_limit_bytes=56 * 1024 * 1024)


def cost(us):
    return pl.CostEstimate(flops=int(us * 1e-6 * 1.1e15), bytes_accessed=int(us * 1e-6 * 3.3e12), transcendentals=0)


def pack_kernel(*refs):
    o_ref = refs[-1]
    for n, x_ref in enumerate(refs[:-1]):
        for h in range(8):
            o_ref[h, n] = x_ref[:, :, :, h * HEAD_DIM : (h + 1) * HEAD_DIM].reshape(CHUNK)


def pack(*bands):
    count = len(bands)
    return pl.pallas_call(
        pack_kernel,
        grid=(2,),
        in_specs=[pl.BlockSpec((3, 3, 24, 1024), lambda j: (0, 0, 0, j))] * count,
        out_specs=pl.BlockSpec((8, count) + CHUNK, lambda j: (j, 0, 0, 0, 0)),
        out_shape=jax.ShapeDtypeStruct((HEADS, count) + CHUNK, BF16),
        compiler_params=params(),
        cost_estimate=cost(2 * count),
        name="pack",
    )(*bands)


def unpack_kernel(x_ref, o_ref):
    for h in range(8):
        o_ref[:, :, :, h * HEAD_DIM : (h + 1) * HEAD_DIM] = x_ref[h].reshape(3, 3, 24, HEAD_DIM)


def unpack(x):
    return pl.pallas_call(
        unpack_kernel,
        grid=(2,),
        in_specs=[pl.BlockSpec((8,) + CHUNK, lambda j: (j, 0, 0, 0))],
        out_specs=pl.BlockSpec((3, 3, 24, 1024), lambda j: (0, 0, 0, j)),
        out_shape=jax.ShapeDtypeStruct((3, 3, 24, HEADS * HEAD_DIM), BF16),
        compiler_params=params(),
        cost_estimate=cost(2),
        name="unpack",
    )(x)


def assemble_kernel(cuts, got_ref, *o_refs):
    for b in range(3):
        n = [b in cut for cut in cuts].index(True)
        for m in range(got_ref.shape[1]):
            for half in range(2):
                slabs = [
                    got_ref[half * 8 + row // 3, m, f * 3 + row % 3].astype(F32)
                    for f in range(3)
                    for row in range(8 * b, 8 * b + 8)
                ]
                for c in range(3):
                    tokens = jnp.concatenate([s[c * 8 : (c + 1) * 8] for s in slabs], axis=0)
                    o_refs[n][m, b - cuts[n][0], c, half * HALF : (half + 1) * HALF] = tokens.astype(BF16)


def assemble(got, first, count, cuts):
    shapes = [(count, len(cut), 3, BLOCK, HEAD_DIM) for cut in cuts]
    whole = lambda shape: pl.BlockSpec(shape, lambda i, n=len(shape): (0,) * n)
    return pl.pallas_call(
        functools.partial(assemble_kernel, cuts),
        grid=(1,),
        in_specs=[pl.BlockSpec((16, count) + CHUNK, lambda i: (0, first // count, 0, 0, 0))],
        out_specs=[whole(s) for s in shapes],
        out_shape=[jax.ShapeDtypeStruct(s, BF16) for s in shapes],
        compiler_params=params(),
        cost_estimate=cost(2 * count),
        name="assemble",
    )(got)


def near(n):
    return range(max(n - 1, 0), min(n + 1, 2) + 1)


def groups(q_bands, k_bands):
    if k_bands == [0, 1, 2]:
        return [((0, 1), (0, 1)), ((1, 2), (2,)), ((2,), (1,))]
    if k_bands == [0, 1]:
        return [((0, 1), (0, 1)), ((2,), (1,))]
    return [(tuple(q_bands), tuple(k_bands))]


def attend_kernel(plan, *refs):
    own, last, cuts, q_bands = plan
    refs = list(refs)
    sides = 1 if own else 2
    flag_ref = None if own else refs.pop(0)
    q_ref = refs.pop(0)
    kv = [{}, {}]
    for side in range(sides):
        for cut in cuts:
            ref = refs.pop(0)
            for p in cut:
                kv[side][p] = (ref, p - cut[0])
    k_bands = [p for cut in cuts for p in cut]
    if not own:
        acc_in, row_in = refs.pop(0), refs.pop(0)
    if last:
        o_ref = refs.pop(0)
    acc_out, row_out = refs

    def tile(which, side, p, c):
        ref, at = kv[side][p]
        return ref[which, at, c]

    def run(which, places, cols):
        wide = len(cols) * BLOCK
        parts = []
        for p, side in places:
            ref, at = kv[side][p]
            parts.append(ref[which, at, cols[0] : cols[-1] + 1].reshape(wide, HEAD_DIM))
        return jnp.concatenate(parts, axis=0)

    worst = jnp.zeros((1, BLOCK), F32)
    for b in range(3):
        if b not in q_bands:
            for c in range(3):
                acc_out[3 * b + c] = acc_in[3 * b + c]
                row_out[3 * b + c] = row_in[3 * b + c]
    for c in range(3):
        cols = list(near(c))
        wide = len(cols) * BLOCK
        accs, totals, tops = {}, {}, {}
        if not own:
            for b in q_bands:
                at = 3 * b + c
                accs[b], totals[b], tops[b] = acc_in[at], row_in[at, 0:1], row_in[at, 1:2]
        for bands, keys in groups(q_bands, k_bands):
            places = [(p, side) for p in keys for side in range(sides)]
            q = jnp.concatenate([q_ref[0, b, c] for b in bands], axis=0)
            scores = lax.dot_general(run(0, places, cols), q, NT, preferred_element_type=F32)
            for n, b in enumerate(bands):
                if b not in tops:
                    mine = (places.index((b, 0)) * len(cols) + cols.index(c)) * BLOCK
                    mine = scores[mine : mine + BLOCK, n * BLOCK : (n + 1) * BLOCK]
                    tops[b] = jnp.max(mine, axis=0, keepdims=True) * SCORE_SCALE
            top = jnp.concatenate([tops[b] for b in bands], axis=1)
            shifts = [top] if own else [top + (1 - flag_ref[side]).astype(F32) * 1e30 for side in range(sides)]
            weights = jnp.concatenate(
                [
                    jnp.exp2(scores[n * wide : (n + 1) * wide] * SCORE_SCALE - shifts[side]).astype(BF16)
                    for n, (p, side) in enumerate(places)
                ],
                axis=0,
            )
            values = run(1, places, cols)
            values = jnp.concatenate([values.T, jnp.ones((16, values.shape[0]), BF16)], axis=0)
            both = jnp.dot(values, weights, preferred_element_type=F32)
            for n, b in enumerate(bands):
                here = both[:, n * BLOCK : (n + 1) * BLOCK]
                acc, total = here[:HEAD_DIM], here[HEAD_DIM : HEAD_DIM + 1]
                accs[b] = accs[b] + acc if b in accs else acc
                totals[b] = totals[b] + total if b in totals else total
        for b in q_bands:
            at = 3 * b + c
            acc_out[at] = accs[b]
            row_out[at] = jnp.concatenate([totals[b], tops[b], jnp.zeros((6, BLOCK), F32)], axis=0)
            worst = jnp.maximum(worst, jnp.where(totals[b] < OVER, 0.0, 1.0))

    @pl.when(jnp.max(worst) > 0.0)
    def _():
        for b in q_bands:

            def redo(c, carry, b=b):
                at = 3 * b + c
                q = q_ref[0, b, c]
                if own:
                    acc_out[at] = jnp.zeros((HEAD_DIM, BLOCK), F32)
                    row_out[at, 0:1] = jnp.zeros((1, BLOCK), F32)
                    row_out[at, 1:2] = jnp.full((1, BLOCK), LOWEST, F32)
                else:
                    acc_out[at] = acc_in[at]
                    row_out[at] = row_in[at]
                for side in range(sides):
                    for p in k_bands:
                        if p not in near(b):
                            continue

                        def some(k, carry, side=side, p=p):
                            scores = lax.dot_general(tile(0, side, p, k), q, NT, preferred_element_type=F32)
                            before = row_out[at, 1:2]
                            top = jnp.maximum(before, jnp.max(scores, axis=0, keepdims=True) * SCORE_SCALE)
                            weights = jnp.exp2(scores * SCORE_SCALE - top)
                            fade = jnp.exp2(before - top)
                            acc = lax.dot_general(
                                tile(1, side, p, k), weights.astype(BF16), TN, preferred_element_type=F32
                            )
                            acc_out[at] = acc_out[at] * fade + acc
                            row_out[at, 0:1] = row_out[at, 0:1] * fade + jnp.sum(weights, axis=0, keepdims=True)
                            row_out[at, 1:2] = top
                            return carry

                        low, high = jnp.maximum(c - 1, 0), jnp.minimum(c + 1, 2) + 1
                        if own:
                            lax.fori_loop(low, high, some, 0)
                        else:

                            @pl.when(flag_ref[side] != 0)
                            def _(some=some, low=low, high=high):
                                lax.fori_loop(low, high, some, 0)

                return carry

            lax.fori_loop(0, 3, redo, 0)

    if last:
        for b in range(3):
            tiles = [(acc_out[3 * b + c] / row_out[3 * b + c, 0:1]).T for c in range(3)]
            for half in range(2):
                for f in range(3):
                    for n in range(8):
                        row = 8 * b + n
                        at = half * HALF + f * 64 + n * 8
                        slab = jnp.concatenate([t[at : at + 8] for t in tiles], axis=0)
                        o_ref[half * 8 + row // 3, f * 3 + row % 3] = slab.astype(BF16)


ACC = (9, HEAD_DIM, BLOCK)
ROW = (9, 8, BLOCK)


def attend(queries, keys_values, cuts, flags=None, state=None, last=False, us=12):
    own = state is None
    k_bands = [p for cut in cuts for p in cut]
    q_bands = [b for b in range(3) if any(p in near(b) for p in k_bands)]
    operands = [queries] + [a for side in keys_values for a in side]
    in_specs = []
    if not own:
        operands = [flags] + operands + list(state)
        in_specs.append(pl.BlockSpec(memory_space=pltpu.SMEM))
    in_specs += [pl.BlockSpec(memory_space=pltpu.VMEM)] * (len(operands) - len(in_specs))
    state_shapes = [jax.ShapeDtypeStruct(ACC, F32), jax.ShapeDtypeStruct(ROW, F32)]
    if last:
        out_shape = [jax.ShapeDtypeStruct((16,) + CHUNK, BF16)]
        scratch = [pltpu.VMEM(s.shape, F32) for s in state_shapes]
    else:
        out_shape, scratch = state_shapes, []
    return pl.pallas_call(
        functools.partial(attend_kernel, (own, last, cuts, q_bands)),
        in_specs=in_specs,
        out_specs=[pl.BlockSpec(memory_space=pltpu.VMEM)] * len(out_shape),
        out_shape=out_shape,
        scratch_shapes=scratch,
        compiler_params=params(),
        cost_estimate=cost(us),
        name="attend",
    )(*operands)


PLANE = ("core", "z", "yhi")


def exchange(x):
    return lax.all_to_all(x, PLANE, 0, 0, tiled=True)


def from_tile(x, steps):
    return lax.ppermute(x, ("ylo", "x"), [(t, t + steps) for t in range(8) if 0 <= t + steps < 8])


CUTS = ((0, 1), (2,))


def body(query_band, key_band, value_band):
    tile = (lax.axis_index("ylo") * 4 + lax.axis_index("x")).astype(jnp.int32)
    flags = jnp.stack([tile > 0, tile < 7]).astype(jnp.int32)
    got = exchange(pack(key_band, value_band, query_band))
    here = assemble(got, 0, 2, CUTS)
    near_first = [from_tile(here[0], s) for s in (1, -1)]
    (queries,) = assemble(got, 2, 1, ((0, 1, 2),))
    state = attend(queries, [here], CUTS, us=12)
    second, state = lax.optimization_barrier((here[1], state))
    near_second = [from_tile(second, s) for s in (1, -1)]
    state = attend(queries, [[a] for a in near_first], CUTS[:1], flags, state, us=15)
    state = attend(queries, [[a] for a in near_second], CUTS[1:], flags, state, last=True, us=8)
    return unpack(exchange(state[0]))


def solution(mesh):
    split = Mesh(mesh.devices.reshape(2, 4, 2, 4, 2), ("ylo", "x", "core", "z", "yhi"))
    spec = P(("ylo", "x", "core"), ("z", "yhi"), None, None)
    return jax.shard_map(body, mesh=split, in_specs=(spec, spec, spec), out_specs=spec, check_vma=False)
```

```python
import functools

import jax
import jax.numpy as jnp
from jax import lax
from jax.experimental import pallas as pl
from jax.experimental.pallas import tpu as pltpu
from jax.sharding import Mesh, PartitionSpec as P

HEAD_DIM = 128
HEADS = 16
BLOCK = 384
HALF = 192
SCORE_SCALE = HEAD_DIM ** (-0.5) * 1.4426950408889634
LOWEST = -1e30
OVER = 2.0**100
BF16 = jnp.bfloat16
F32 = jnp.float32
CHUNK = (9, 24, HEAD_DIM)
NT = (((1,), (1,)), ((), ()))
TN = (((0,), (0,)), ((), ()))


def params(mib):
    return pltpu.CompilerParams(vmem_limit_bytes=mib * 1024 * 1024)


def cost(us):
    return pl.CostEstimate(flops=int(us * 1e6), bytes_accessed=int(us * 1e4), transcendentals=0)


def pack_first_kernel(core_ref, *refs):
    o_ref = refs[-1]
    for n, x_ref in enumerate(refs[:-1]):
        for h in range(8):
            o_ref[h, n] = x_ref[:, :, 0:16, h * HEAD_DIM : (h + 1) * HEAD_DIM].reshape(9, 16, HEAD_DIM)


def pack_second_kernel(core_ref, key_ref, value_ref, query_ref, o_ref):
    for h in range(8):
        lanes = slice(h * HEAD_DIM, (h + 1) * HEAD_DIM)
        for n in range(9):
            last = [ref[n // 3, n % 3, 16:24, lanes].astype(F32) for ref in (key_ref, value_ref)]
            o_ref[h, n, 0:16] = jnp.concatenate(last, axis=0).astype(BF16)
            o_ref[h, n, 16:40] = query_ref[n // 3, n % 3, :, lanes]


def pack(core, kernel, inner, *bands):
    return pl.pallas_call(
        kernel,
        grid_spec=pltpu.PrefetchScalarGridSpec(
            num_scalar_prefetch=1,
            grid=(2,),
            in_specs=[pl.BlockSpec((3, 3, 24, 1024), lambda j, s: (0, 0, 0, (j + s[0]) % 2))] * len(bands),
            out_specs=pl.BlockSpec((8,) + inner, lambda j, s: (j,) + (0,) * len(inner)),
        ),
        out_shape=jax.ShapeDtypeStruct((HEADS,) + inner, BF16),
        compiler_params=params(56),
        cost_estimate=cost(1.2 * len(bands)),
        name="pack",
    )(core, *bands)


FIRST = (2, 9, 16, HEAD_DIM)
SECOND = (9, 40, HEAD_DIM)


def unpack_kernel(core_ref, x_ref, o_ref):
    for h in range(8):
        o_ref[:, :, :, h * HEAD_DIM : (h + 1) * HEAD_DIM] = x_ref[h].reshape(3, 3, 24, HEAD_DIM)


def unpack(core, x):
    return pl.pallas_call(
        unpack_kernel,
        grid_spec=pltpu.PrefetchScalarGridSpec(
            num_scalar_prefetch=1,
            grid=(2,),
            in_specs=[pl.BlockSpec((8,) + CHUNK, lambda j, s: (j, 0, 0, 0))],
            out_specs=pl.BlockSpec((3, 3, 24, 1024), lambda j, s: (0, 0, 0, (j + s[0]) % 2)),
        ),
        out_shape=jax.ShapeDtypeStruct((3, 3, 24, HEADS * HEAD_DIM), BF16),
        compiler_params=params(12),
        cost_estimate=cost(1),
        name="unpack",
    )(core, x)


def gather(o_refs, slab):
    for b in range(3):
        for half in range(2):
            slabs = [slab(half, row // 3, f * 3 + row % 3) for f in range(3) for row in range(8 * b, 8 * b + 8)]
            for c, (ref, where) in enumerate(o_refs):
                tokens = jnp.concatenate([s[c * 8 : (c + 1) * 8] for s in slabs], axis=0)
                ref[where + (b, pl.ds(half * HALF, HALF))] = tokens.astype(BF16)


def assemble_first_kernel(kept_ref, came_ref, kv_ref):
    halves = (kept_ref, came_ref)
    for m in range(2):
        places = [(kv_ref, (m, c)) for c in range(2)]
        gather(places, lambda half, chunk, n, m=m: halves[half][chunk, m, n].astype(F32))


def assemble_second_kernel(kept_ref, came_ref, kv_ref):
    halves = (kept_ref, came_ref)
    places = [(kv_ref, (m, 0)) for m in range(2)]
    gather(places, lambda half, chunk, n: halves[half][chunk, n, 0:16].astype(F32))


def assemble_queries_kernel(kept_ref, came_ref, q_ref):
    places = [(q_ref, (0, c)) for c in range(3)]
    slab = lambda half, chunk, n: (came_ref[chunk, n] if half else kept_ref[chunk, n, 16:40]).astype(F32)
    gather(places, slab)


def assemble(kernel, got, came, *leads):
    return pl.pallas_call(
        kernel,
        in_specs=[pl.BlockSpec(memory_space=pltpu.VMEM)] * 2,
        out_specs=[pl.BlockSpec(memory_space=pltpu.VMEM)] * len(leads),
        out_shape=[jax.ShapeDtypeStruct(lead + (3, BLOCK, HEAD_DIM), BF16) for lead in leads],
        compiler_params=params(8),
        cost_estimate=cost(1),
        name="assemble",
    )(got, came)


def near(n):
    return range(max(n - 1, 0), min(n + 1, 2) + 1)


def groups(q_bands, k_bands):
    if k_bands == [0, 1, 2]:
        return [((0, 1), (0, 1)), ((1, 2), (2,)), ((2,), (1,))]
    if k_bands == [0, 1]:
        return [((0, 1), (0, 1)), ((2,), (1,))]
    return [(tuple(q_bands), tuple(k_bands))]


def attend_kernel(plan, *refs):
    own, last, cuts, q_bands = plan
    refs = list(refs)
    sides = 1 if own else 2
    flag_ref = None if own else refs.pop(0)
    q_ref = refs.pop(0)
    kv = [{}, {}]
    for side in range(sides):
        for cut in cuts:
            ref = refs.pop(0)
            for p in cut:
                kv[side][p] = (ref, p - cut[0])
    k_bands = [p for cut in cuts for p in cut]
    if not own:
        acc_in, row_in = refs.pop(0), refs.pop(0)
    if last:
        o_refs = (refs.pop(0), refs.pop(0))
    acc_out, row_out = refs

    def tile(which, side, p, c):
        ref, at = kv[side][p]
        return ref[which, at, c]

    def run(which, places, cols):
        wide = len(cols) * BLOCK
        parts = []
        for p, side in places:
            ref, at = kv[side][p]
            parts.append(ref[which, at, cols[0] : cols[-1] + 1].reshape(wide, HEAD_DIM))
        return jnp.concatenate(parts, axis=0)

    worst = jnp.zeros((1, BLOCK), F32)
    for b in range(3):
        if b not in q_bands:
            for c in range(3):
                acc_out[3 * b + c] = acc_in[3 * b + c]
                row_out[3 * b + c] = row_in[3 * b + c]
    for c in range(3):
        cols = list(near(c))
        wide = len(cols) * BLOCK
        accs, totals, tops = {}, {}, {}
        if not own:
            for b in q_bands:
                at = 3 * b + c
                accs[b], totals[b], tops[b] = acc_in[at], row_in[at, 0:1], row_in[at, 1:2]
        for bands, keys in groups(q_bands, k_bands):
            places = [(p, side) for p in keys for side in range(sides)]
            q = jnp.concatenate([q_ref[0, b, c] for b in bands], axis=0)
            scores = lax.dot_general(run(0, places, cols), q, NT, preferred_element_type=F32)
            for n, b in enumerate(bands):
                if b not in tops:
                    mine = (places.index((b, 0)) * len(cols) + cols.index(c)) * BLOCK
                    mine = scores[mine : mine + BLOCK, n * BLOCK : (n + 1) * BLOCK]
                    tops[b] = jnp.max(mine, axis=0, keepdims=True) * SCORE_SCALE
            top = jnp.concatenate([tops[b] for b in bands], axis=1)
            shifts = [top] if own else [top + (1 - flag_ref[side]).astype(F32) * 1e30 for side in range(sides)]
            weights = jnp.concatenate(
                [
                    jnp.exp2(scores[n * wide : (n + 1) * wide] * SCORE_SCALE - shifts[side]).astype(BF16)
                    for n, (p, side) in enumerate(places)
                ],
                axis=0,
            )
            values = run(1, places, cols)
            values = jnp.concatenate([values.T, jnp.ones((16, values.shape[0]), BF16)], axis=0)
            both = jnp.dot(values, weights, preferred_element_type=F32)
            for n, b in enumerate(bands):
                here = both[:, n * BLOCK : (n + 1) * BLOCK]
                acc, total = here[:HEAD_DIM], here[HEAD_DIM : HEAD_DIM + 1]
                accs[b] = accs[b] + acc if b in accs else acc
                totals[b] = totals[b] + total if b in totals else total
        for b in q_bands:
            at = 3 * b + c
            acc_out[at] = accs[b]
            row_out[at] = jnp.concatenate([totals[b], tops[b], jnp.zeros((6, BLOCK), F32)], axis=0)
            worst = jnp.maximum(worst, jnp.where(totals[b] < OVER, 0.0, 1.0))

    @pl.when(jnp.max(worst) > 0.0)
    def _():
        for b in q_bands:

            def redo(c, carry, b=b):
                at = 3 * b + c
                q = q_ref[0, b, c]
                if own:
                    acc_out[at] = jnp.zeros((HEAD_DIM, BLOCK), F32)
                    row_out[at, 0:1] = jnp.zeros((1, BLOCK), F32)
                    row_out[at, 1:2] = jnp.full((1, BLOCK), LOWEST, F32)
                else:
                    acc_out[at] = acc_in[at]
                    row_out[at] = row_in[at]
                for side in range(sides):
                    for p in k_bands:
                        if p not in near(b):
                            continue

                        def some(k, carry, side=side, p=p):
                            scores = lax.dot_general(tile(0, side, p, k), q, NT, preferred_element_type=F32)
                            before = row_out[at, 1:2]
                            top = jnp.maximum(before, jnp.max(scores, axis=0, keepdims=True) * SCORE_SCALE)
                            weights = jnp.exp2(scores * SCORE_SCALE - top)
                            fade = jnp.exp2(before - top)
                            acc = lax.dot_general(
                                tile(1, side, p, k), weights.astype(BF16), TN, preferred_element_type=F32
                            )
                            acc_out[at] = acc_out[at] * fade + acc
                            row_out[at, 0:1] = row_out[at, 0:1] * fade + jnp.sum(weights, axis=0, keepdims=True)
                            row_out[at, 1:2] = top
                            return carry

                        low, high = jnp.maximum(c - 1, 0), jnp.minimum(c + 1, 2) + 1
                        if own:
                            lax.fori_loop(low, high, some, 0)
                        else:

                            @pl.when(flag_ref[side] != 0)
                            def _(some=some, low=low, high=high):
                                lax.fori_loop(low, high, some, 0)

                return carry

            lax.fori_loop(0, 3, redo, 0)

    if last:
        for b in range(3):
            tiles = [(acc_out[3 * c + b] / row_out[3 * c + b, 0:1]).T for c in range(3)]
            for half in range(2):
                for f in range(3):
                    for n in range(8):
                        row = 8 * b + n
                        at = half * HALF + f * 64 + n * 8
                        slab = jnp.concatenate([t[at : at + 8] for t in tiles], axis=0)
                        o_refs[half][row // 3, f * 3 + row % 3] = slab.astype(BF16)


ACC = (9, HEAD_DIM, BLOCK)
ROW = (9, 8, BLOCK)


def attend(queries, keys_values, cuts, flags=None, state=None, last=False, us=12):
    own = state is None
    k_bands = [p for cut in cuts for p in cut]
    q_bands = [b for b in range(3) if any(p in near(b) for p in k_bands)]
    operands = [queries] + [a for side in keys_values for a in side]
    in_specs = []
    if not own:
        operands = [flags] + operands + list(state)
        in_specs.append(pl.BlockSpec(memory_space=pltpu.SMEM))
    in_specs += [pl.BlockSpec(memory_space=pltpu.VMEM)] * (len(operands) - len(in_specs))
    state_shapes = [jax.ShapeDtypeStruct(ACC, F32), jax.ShapeDtypeStruct(ROW, F32)]
    if last:
        out_shape = [jax.ShapeDtypeStruct((8,) + CHUNK, BF16)] * 2
        scratch = [pltpu.VMEM(s.shape, F32) for s in state_shapes]
    else:
        out_shape, scratch = state_shapes, []
    return pl.pallas_call(
        functools.partial(attend_kernel, (own, last, cuts, q_bands)),
        in_specs=in_specs,
        out_specs=[pl.BlockSpec(memory_space=pltpu.VMEM)] * len(out_shape),
        out_shape=out_shape,
        scratch_shapes=scratch,
        compiler_params=params(24),
        cost_estimate=cost(us),
        name="attend",
    )(*operands)


PLANE = ("ylo", "core", "z", "yhi")


def plane_groups():
    at = lambda ylo, core, n: (ylo * 2 + core) * 8 + n
    return [[at(ylo, core, n) for ylo in (core, 1 - core) for n in range(8)] for core in (0, 1)]


def exchange(x):
    return lax.all_to_all(x, PLANE, 0, 0, axis_index_groups=plane_groups(), tiled=True)


def swap_cores(x):
    return lax.ppermute(x, "core", [(0, 1), (1, 0)])


def from_tile(x, steps):
    at = lambda tile: (tile % 4) * 2 + tile // 4
    return lax.ppermute(x, ("x", "core"), [(at(t), at(t + steps)) for t in range(8) if 0 <= t + steps < 8])


CUTS = ((0, 1), (2,))


def body(query_band, key_band, value_band):
    core_index = lax.axis_index("core").astype(jnp.int32)
    core = core_index.reshape(1)
    tile = core_index * 4 + lax.axis_index("x").astype(jnp.int32)
    flags = jnp.stack([tile > 0, tile < 7]).astype(jnp.int32)
    got = exchange(pack(core, pack_first_kernel, FIRST, key_band, value_band))
    rest = pack(core, pack_second_kernel, SECOND, key_band, value_band, query_band)
    rest, got = lax.optimization_barrier((rest, got))
    came = swap_cores(got[8:])
    got_rest = exchange(rest)
    (first,) = assemble(assemble_first_kernel, got, came, (2, 2))
    near_first = [from_tile(first, s) for s in (1, -1)]
    (second,) = assemble(assemble_second_kernel, got_rest, swap_cores(got_rest[8:, :, :16]), (2, 1))
    (queries,) = assemble(assemble_queries_kernel, got_rest, swap_cores(got_rest[8:, :, 16:]), (1, 3))
    near_second = [from_tile(second, s) for s in (1, -1)]
    state = attend(queries, [[first, second]], CUTS, us=9)
    state = attend(queries, [[a] for a in near_first], CUTS[:1], flags, state, us=10)
    kept, sent = attend(queries, [[a] for a in near_second], CUTS[1:], flags, state, last=True, us=5)
    back = jnp.concatenate([kept, swap_cores(sent)], axis=0)
    return unpack(core, exchange(back))


def solution(mesh):
    split = Mesh(mesh.devices.reshape(2, 4, 2, 4, 2), ("ylo", "x", "core", "z", "yhi"))
    spec = P(("ylo", "x", "core"), ("z", "yhi"), None, None)
    return jax.shard_map(body, mesh=split, in_specs=(spec, spec, spec), out_specs=spec, check_vma=False)
```

```python
import functools

import jax
import jax.numpy as jnp
from jax import lax
from jax.experimental import pallas as pl
from jax.experimental.pallas import tpu as pltpu
from jax.sharding import Mesh, PartitionSpec as P

HEAD_DIM = 128
HEADS = 16
BLOCK = 384
HALF = 192
SCORE_SCALE = HEAD_DIM ** (-0.5) * 1.4426950408889634
LOWEST = -1e30
OVER = 2.0**100
BF16 = jnp.bfloat16
F32 = jnp.float32
CHUNK = (9, 24, HEAD_DIM)
NT = (((1,), (1,)), ((), ()))
TN = (((0,), (0,)), ((), ()))


def params(mib):
    return pltpu.CompilerParams(vmem_limit_bytes=mib * 1024 * 1024)


def cost(us):
    return pl.CostEstimate(flops=int(us * 1e6), bytes_accessed=int(us * 1e4), transcendentals=0)


def pack_first_kernel(core_ref, *refs):
    o_ref = refs[-1]
    for n, x_ref in enumerate(refs[:-1]):
        for h in range(8):
            o_ref[h, n] = x_ref[:, :, :, h * HEAD_DIM : (h + 1) * HEAD_DIM].reshape(9, 16, HEAD_DIM)


def pack_second_kernel(core_ref, key_ref, value_ref, query_ref, o_ref):
    for h in range(8):
        lanes = slice(h * HEAD_DIM, (h + 1) * HEAD_DIM)
        for n in range(9):
            last = [ref[n // 3, n % 3, 16:24, lanes].astype(F32) for ref in (key_ref, value_ref)]
            o_ref[h, n, 0:16] = jnp.concatenate(last, axis=0).astype(BF16)
            o_ref[h, n, 16:40] = query_ref[n // 3, n % 3, :, lanes]


def pack(core, kernel, columns, inner, *bands):
    return pl.pallas_call(
        kernel,
        grid_spec=pltpu.PrefetchScalarGridSpec(
            num_scalar_prefetch=1,
            grid=(2,),
            in_specs=[pl.BlockSpec((3, 3, columns, 1024), lambda j, s: (0, 0, 0, (j + s[0]) % 2))] * len(bands),
            out_specs=pl.BlockSpec((8,) + inner, lambda j, s: (j,) + (0,) * len(inner)),
        ),
        out_shape=jax.ShapeDtypeStruct((HEADS,) + inner, BF16),
        compiler_params=params(56),
        cost_estimate=cost(1.2 * len(bands)),
        name="pack",
    )(core, *bands)


FIRST = (2, 9, 16, HEAD_DIM)
SECOND = (9, 40, HEAD_DIM)


def unpack_kernel(core_ref, x_ref, o_ref):
    for h in range(8):
        o_ref[:, :, :, h * HEAD_DIM : (h + 1) * HEAD_DIM] = x_ref[h].reshape(3, 3, 24, HEAD_DIM)


def unpack(core, x):
    return pl.pallas_call(
        unpack_kernel,
        grid_spec=pltpu.PrefetchScalarGridSpec(
            num_scalar_prefetch=1,
            grid=(2,),
            in_specs=[pl.BlockSpec((8,) + CHUNK, lambda j, s: (j, 0, 0, 0))],
            out_specs=pl.BlockSpec((3, 3, 24, 1024), lambda j, s: (0, 0, 0, (j + s[0]) % 2)),
        ),
        out_shape=jax.ShapeDtypeStruct((3, 3, 24, HEADS * HEAD_DIM), BF16),
        compiler_params=params(12),
        cost_estimate=cost(1),
        name="unpack",
    )(core, x)


def gather(o_refs, slab):
    for b in range(3):
        for half in range(2):
            slabs = [slab(half, row // 3, f * 3 + row % 3) for f in range(3) for row in range(8 * b, 8 * b + 8)]
            for c, (ref, where) in enumerate(o_refs):
                tokens = jnp.concatenate([s[c * 8 : (c + 1) * 8] for s in slabs], axis=0)
                ref[where + (b, pl.ds(half * HALF, HALF))] = tokens.astype(BF16)


def assemble_first_kernel(kept_ref, came_ref, kv_ref):
    halves = (kept_ref, came_ref)
    for m in range(2):
        places = [(kv_ref, (m, c)) for c in range(2)]
        gather(places, lambda half, chunk, n, m=m: halves[half][chunk, m, n].astype(F32))


def assemble_second_kernel(kept_ref, came_ref, kv_ref):
    halves = (kept_ref, came_ref)
    places = [(kv_ref, (m, 0)) for m in range(2)]
    gather(places, lambda half, chunk, n: halves[half][chunk, n, 0:16].astype(F32))


def assemble_queries_kernel(kept_ref, came_ref, q_ref):
    places = [(q_ref, (0, c)) for c in range(3)]
    slab = lambda half, chunk, n: (came_ref[chunk, n] if half else kept_ref[chunk, n, 16:40]).astype(F32)
    gather(places, slab)


def assemble(kernel, got, came, *leads):
    return pl.pallas_call(
        kernel,
        in_specs=[pl.BlockSpec(memory_space=pltpu.VMEM)] * 2,
        out_specs=[pl.BlockSpec(memory_space=pltpu.VMEM)] * len(leads),
        out_shape=[jax.ShapeDtypeStruct(lead + (3, BLOCK, HEAD_DIM), BF16) for lead in leads],
        compiler_params=params(8),
        cost_estimate=cost(1),
        name="assemble",
    )(got, came)


def near(n):
    return range(max(n - 1, 0), min(n + 1, 2) + 1)


def groups(q_bands, k_bands):
    if k_bands == [0, 1, 2]:
        return [((0, 1), (0, 1)), ((1, 2), (2,)), ((2,), (1,))]
    if k_bands == [0, 1]:
        return [((0, 1), (0, 1)), ((2,), (1,))]
    return [(tuple(q_bands), tuple(k_bands))]


def attend_kernel(plan, *refs):
    own, last, cuts, q_bands = plan
    refs = list(refs)
    sides = 1 if own else 2
    flag_ref = None if own else refs.pop(0)
    q_ref = refs.pop(0)
    kv = [{}, {}]
    for side in range(sides):
        for cut in cuts:
            ref = refs.pop(0)
            for p in cut:
                kv[side][p] = (ref, p - cut[0])
    k_bands = [p for cut in cuts for p in cut]
    if not own:
        acc_in, row_in = refs.pop(0), refs.pop(0)
    if last:
        o_refs = (refs.pop(0), refs.pop(0))
    acc_out, row_out = refs

    def tile(which, side, p, c):
        ref, at = kv[side][p]
        return ref[which, at, c]

    def run(which, places, cols):
        wide = len(cols) * BLOCK
        parts = []
        for p, side in places:
            ref, at = kv[side][p]
            parts.append(ref[which, at, cols[0] : cols[-1] + 1].reshape(wide, HEAD_DIM))
        return jnp.concatenate(parts, axis=0)

    worst = jnp.zeros((1, BLOCK), F32)
    for b in range(3):
        if b not in q_bands:
            for c in range(3):
                acc_out[3 * b + c] = acc_in[3 * b + c]
                row_out[3 * b + c] = row_in[3 * b + c]
    accs, totals, tops = {}, {}, {}
    tasks = [(c, bands, keys) for c in range(3) for bands, keys in groups(q_bands, k_bands)]
    if not own:
        for c in range(3):
            for b in q_bands:
                at = 3 * b + c
                accs[b, c], totals[b, c], tops[b, c] = acc_in[at], row_in[at, 0:1], row_in[at, 1:2]

    def first_stage(c, bands, keys):
        cols = list(near(c))
        places = [(p, side) for p in keys for side in range(sides)]
        q = jnp.concatenate([q_ref[0, b, c] for b in bands], axis=0)
        scores = lax.dot_general(run(0, places, cols), q, NT, preferred_element_type=F32)
        for n, b in enumerate(bands):
            if (b, c) not in tops:
                mine = (places.index((b, 0)) * len(cols) + cols.index(c)) * BLOCK
                mine = scores[mine : mine + BLOCK, n * BLOCK : (n + 1) * BLOCK]
                tops[b, c] = jnp.max(mine, axis=0, keepdims=True) * SCORE_SCALE
        return scores

    def second_stage(c, bands, keys, scores):
        cols = list(near(c))
        wide = len(cols) * BLOCK
        places = [(p, side) for p in keys for side in range(sides)]
        top = jnp.concatenate([tops[b, c] for b in bands], axis=1)
        shifts = [top] if own else [top + (1 - flag_ref[side]).astype(F32) * 1e30 for side in range(sides)]
        weights = jnp.concatenate(
            [
                jnp.exp2(scores[n * wide : (n + 1) * wide] * SCORE_SCALE - shifts[side]).astype(BF16)
                for n, (p, side) in enumerate(places)
            ],
            axis=0,
        )
        values = run(1, places, cols)
        values = jnp.concatenate([values.T, jnp.ones((16, values.shape[0]), BF16)], axis=0)
        both = jnp.dot(values, weights, preferred_element_type=F32)
        for n, b in enumerate(bands):
            here = both[:, n * BLOCK : (n + 1) * BLOCK]
            acc, total = here[:HEAD_DIM], here[HEAD_DIM : HEAD_DIM + 1]
            accs[b, c] = accs[b, c] + acc if (b, c) in accs else acc
            totals[b, c] = totals[b, c] + total if (b, c) in totals else total

    scores = first_stage(*tasks[0])
    for n, task in enumerate(tasks):
        ahead = first_stage(*tasks[n + 1]) if n + 1 < len(tasks) else None
        second_stage(*task, scores)
        scores = ahead
    for c in range(3):
        for b in q_bands:
            at = 3 * b + c
            acc_out[at] = accs[b, c]
            row_out[at] = jnp.concatenate([totals[b, c], tops[b, c], jnp.zeros((6, BLOCK), F32)], axis=0)
            worst = jnp.maximum(worst, jnp.where(totals[b, c] < OVER, 0.0, 1.0))

    @pl.when(jnp.max(worst) > 0.0)
    def _():
        for b in q_bands:

            def redo(c, carry, b=b):
                at = 3 * b + c
                q = q_ref[0, b, c]
                if own:
                    acc_out[at] = jnp.zeros((HEAD_DIM, BLOCK), F32)
                    row_out[at, 0:1] = jnp.zeros((1, BLOCK), F32)
                    row_out[at, 1:2] = jnp.full((1, BLOCK), LOWEST, F32)
                else:
                    acc_out[at] = acc_in[at]
                    row_out[at] = row_in[at]
                for side in range(sides):
                    for p in k_bands:
                        if p not in near(b):
                            continue

                        def some(k, carry, side=side, p=p):
                            scores = lax.dot_general(tile(0, side, p, k), q, NT, preferred_element_type=F32)
                            before = row_out[at, 1:2]
                            top = jnp.maximum(before, jnp.max(scores, axis=0, keepdims=True) * SCORE_SCALE)
                            weights = jnp.exp2(scores * SCORE_SCALE - top)
                            fade = jnp.exp2(before - top)
                            acc = lax.dot_general(
                                tile(1, side, p, k), weights.astype(BF16), TN, preferred_element_type=F32
                            )
                            acc_out[at] = acc_out[at] * fade + acc
                            row_out[at, 0:1] = row_out[at, 0:1] * fade + jnp.sum(weights, axis=0, keepdims=True)
                            row_out[at, 1:2] = top
                            return carry

                        low, high = jnp.maximum(c - 1, 0), jnp.minimum(c + 1, 2) + 1
                        if own:
                            lax.fori_loop(low, high, some, 0)
                        else:

                            @pl.when(flag_ref[side] != 0)
                            def _(some=some, low=low, high=high):
                                lax.fori_loop(low, high, some, 0)

                return carry

            lax.fori_loop(0, 3, redo, 0)

    if last:
        for b in range(3):
            tiles = [(acc_out[3 * c + b] / row_out[3 * c + b, 0:1]).T for c in range(3)]
            for half in range(2):
                for f in range(3):
                    for n in range(8):
                        row = 8 * b + n
                        at = half * HALF + f * 64 + n * 8
                        slab = jnp.concatenate([t[at : at + 8] for t in tiles], axis=0)
                        o_refs[half][row // 3, f * 3 + row % 3] = slab.astype(BF16)


ACC = (9, HEAD_DIM, BLOCK)
ROW = (9, 8, BLOCK)


def attend(queries, keys_values, cuts, flags=None, state=None, last=False, us=12):
    own = state is None
    k_bands = [p for cut in cuts for p in cut]
    q_bands = [b for b in range(3) if any(p in near(b) for p in k_bands)]
    operands = [queries] + [a for side in keys_values for a in side]
    in_specs = []
    if not own:
        operands = [flags] + operands + list(state)
        in_specs.append(pl.BlockSpec(memory_space=pltpu.SMEM))
    in_specs += [pl.BlockSpec(memory_space=pltpu.VMEM)] * (len(operands) - len(in_specs))
    state_shapes = [jax.ShapeDtypeStruct(ACC, F32), jax.ShapeDtypeStruct(ROW, F32)]
    if last:
        out_shape = [jax.ShapeDtypeStruct((8,) + CHUNK, BF16)] * 2
        scratch = [pltpu.VMEM(s.shape, F32) for s in state_shapes]
    else:
        out_shape, scratch = state_shapes, []
    return pl.pallas_call(
        functools.partial(attend_kernel, (own, last, cuts, q_bands)),
        in_specs=in_specs,
        out_specs=[pl.BlockSpec(memory_space=pltpu.VMEM)] * len(out_shape),
        out_shape=out_shape,
        scratch_shapes=scratch,
        compiler_params=params(24),
        cost_estimate=cost(us),
        name="attend",
    )(*operands)


PLANE = ("ylo", "core", "z", "yhi")


def plane_groups():
    at = lambda ylo, core, n: (ylo * 2 + core) * 8 + n
    return [[at(ylo, core, n) for ylo in (core, 1 - core) for n in range(8)] for core in (0, 1)]


def exchange(x):
    return lax.all_to_all(x, PLANE, 0, 0, axis_index_groups=plane_groups(), tiled=True)


def swap_cores(x):
    return lax.ppermute(x, "core", [(0, 1), (1, 0)])


def from_tile(x, steps):
    at = lambda tile: (tile % 4) * 2 + tile // 4
    return lax.ppermute(x, ("x", "core"), [(at(t), at(t + steps)) for t in range(8) if 0 <= t + steps < 8])


CUTS = ((0, 1), (2,))


def body(query_band, key_band, value_band):
    core_index = lax.axis_index("core").astype(jnp.int32)
    core = core_index.reshape(1)
    tile = core_index * 4 + lax.axis_index("x").astype(jnp.int32)
    flags = jnp.stack([tile > 0, tile < 7]).astype(jnp.int32)
    got = exchange(pack(core, pack_first_kernel, 16, FIRST, key_band, value_band))
    rest = pack(core, pack_second_kernel, 24, SECOND, key_band, value_band, query_band)
    rest, got = lax.optimization_barrier((rest, got))
    came = swap_cores(got[8:])
    got_rest = exchange(rest)
    (first,) = assemble(assemble_first_kernel, got, came, (2, 2))
    near_first = [from_tile(first, s) for s in (1, -1)]
    came_kv, came_q = (swap_cores(got_rest[8:, :, cut]) for cut in (slice(0, 16), slice(16, 40)))
    (second,) = assemble(assemble_second_kernel, got_rest, came_kv, (2, 1))
    (queries,) = assemble(assemble_queries_kernel, got_rest, came_q, (1, 3))
    second, queries = lax.optimization_barrier((second, queries))
    near_second = [from_tile(second, s) for s in (1, -1)]
    state = attend(queries, [[first, second]], CUTS, us=9)
    state = attend(queries, [[a] for a in near_first], CUTS[:1], flags, state, us=10)
    kept, sent = attend(queries, [[a] for a in near_second], CUTS[1:], flags, state, last=True, us=5)
    back = jnp.concatenate([kept, swap_cores(sent)], axis=0)
    return unpack(core, exchange(back))


def solution(mesh):
    split = Mesh(mesh.devices.reshape(2, 4, 2, 4, 2), ("ylo", "x", "core", "z", "yhi"))
    spec = P(("ylo", "x", "core"), ("z", "yhi"), None, None)
    return jax.shard_map(body, mesh=split, in_specs=(spec, spec, spec), out_specs=spec, check_vma=False)
```

```python
import functools

import jax
import jax.numpy as jnp
from jax import lax
from jax.experimental import pallas as pl
from jax.experimental.pallas import tpu as pltpu
from jax.sharding import Mesh, PartitionSpec as P

HEAD_DIM = 128
HEADS = 16
BLOCK = 384
HALF = 192
SCORE_SCALE = HEAD_DIM ** (-0.5) * 1.4426950408889634
LOWEST = -1e30
OVER = 2.0**100
BF16 = jnp.bfloat16
F32 = jnp.float32
CHUNK = (9, 24, HEAD_DIM)
NT = (((1,), (1,)), ((), ()))
TN = (((0,), (0,)), ((), ()))


def params(mib):
    return pltpu.CompilerParams(vmem_limit_bytes=mib * 1024 * 1024)


def cost(us):
    return pl.CostEstimate(flops=int(us * 1e6), bytes_accessed=int(us * 1e4), transcendentals=0)


def pack_first_kernel(core_ref, *refs):
    o_ref = refs[-1]
    for n, x_ref in enumerate(refs[:-1]):
        for h in range(8):
            o_ref[h, n] = x_ref[:, :, :, h * HEAD_DIM : (h + 1) * HEAD_DIM].reshape(9, 16, HEAD_DIM)


def pack_second_kernel(core_ref, key_ref, value_ref, query_ref, o_ref):
    for h in range(8):
        lanes = slice(h * HEAD_DIM, (h + 1) * HEAD_DIM)
        for n in range(9):
            last = [ref[n // 3, n % 3, 16:24, lanes].astype(F32) for ref in (key_ref, value_ref)]
            o_ref[h, n, 0:16] = jnp.concatenate(last, axis=0).astype(BF16)
            o_ref[h, n, 16:40] = query_ref[n // 3, n % 3, :, lanes]


def pack(core, kernel, columns, inner, *bands):
    return pl.pallas_call(
        kernel,
        grid_spec=pltpu.PrefetchScalarGridSpec(
            num_scalar_prefetch=1,
            grid=(2,),
            in_specs=[pl.BlockSpec((3, 3, columns, 1024), lambda j, s: (0, 0, 0, (j + s[0]) % 2))] * len(bands),
            out_specs=pl.BlockSpec((8,) + inner, lambda j, s: (j,) + (0,) * len(inner)),
        ),
        out_shape=jax.ShapeDtypeStruct((HEADS,) + inner, BF16),
        compiler_params=params(56),
        cost_estimate=cost(1.2 * len(bands)),
        name="pack",
    )(core, *bands)


FIRST = (2, 9, 16, HEAD_DIM)
SECOND = (9, 40, HEAD_DIM)


def unpack_kernel(core_ref, x_ref, o_ref):
    for h in range(8):
        o_ref[:, :, :, h * HEAD_DIM : (h + 1) * HEAD_DIM] = x_ref[h].reshape(3, 3, 24, HEAD_DIM)


def unpack(core, x):
    return pl.pallas_call(
        unpack_kernel,
        grid_spec=pltpu.PrefetchScalarGridSpec(
            num_scalar_prefetch=1,
            grid=(2,),
            in_specs=[pl.BlockSpec((8,) + CHUNK, lambda j, s: (j, 0, 0, 0))],
            out_specs=pl.BlockSpec((3, 3, 24, 1024), lambda j, s: (0, 0, 0, (j + s[0]) % 2)),
        ),
        out_shape=jax.ShapeDtypeStruct((3, 3, 24, HEADS * HEAD_DIM), BF16),
        compiler_params=params(12),
        cost_estimate=cost(1),
        name="unpack",
    )(core, x)


def gather(o_refs, slab):
    for b in range(3):
        for half in range(2):
            slabs = [slab(half, row // 3, f * 3 + row % 3) for f in range(3) for row in range(8 * b, 8 * b + 8)]
            for c, (ref, where) in enumerate(o_refs):
                tokens = jnp.concatenate([s[c * 8 : (c + 1) * 8] for s in slabs], axis=0)
                ref[where + (b, pl.ds(half * HALF, HALF))] = tokens.astype(BF16)


def assemble_first_kernel(kept_ref, came_ref, kv_ref):
    halves = (kept_ref, came_ref)
    for m in range(2):
        places = [(kv_ref, (m, c)) for c in range(2)]
        gather(places, lambda half, chunk, n, m=m: halves[half][chunk, m, n].astype(F32))


def assemble_second_kernel(kept_ref, came_ref, kv_ref):
    halves = (kept_ref, came_ref)
    places = [(kv_ref, (m, 0)) for m in range(2)]
    gather(places, lambda half, chunk, n: halves[half][chunk, n, 0:16].astype(F32))


def assemble_queries_kernel(kept_ref, came_ref, q_ref):
    places = [(q_ref, (0, c)) for c in range(3)]
    slab = lambda half, chunk, n: (came_ref[chunk, n] if half else kept_ref[chunk, n, 16:40]).astype(F32)
    gather(places, slab)


def assemble(kernel, got, came, *leads):
    return pl.pallas_call(
        kernel,
        in_specs=[pl.BlockSpec(memory_space=pltpu.VMEM)] * 2,
        out_specs=[pl.BlockSpec(memory_space=pltpu.VMEM)] * len(leads),
        out_shape=[jax.ShapeDtypeStruct(lead + (3, BLOCK, HEAD_DIM), BF16) for lead in leads],
        compiler_params=params(8),
        cost_estimate=cost(1),
        name="assemble",
    )(got, came)


def near(n):
    return range(max(n - 1, 0), min(n + 1, 2) + 1)


def groups(q_bands, k_bands):
    if k_bands == [0, 1, 2]:
        return [((0, 1), (0,)), ((0, 1, 2), (1,)), ((1, 2), (2,))]
    if k_bands == [0, 1]:
        return [((0, 1), (0, 1)), ((2,), (1,))]
    return [(tuple(q_bands), tuple(k_bands))]


def attend_kernel(plan, *refs):
    own, last, cuts, q_bands = plan
    refs = list(refs)
    sides = 1 if own else 2
    flag_ref = None if own else refs.pop(0)
    q_ref = refs.pop(0)
    kv = [{}, {}]
    for side in range(sides):
        for cut in cuts:
            ref = refs.pop(0)
            for p in cut:
                kv[side][p] = (ref, p - cut[0])
    k_bands = [p for cut in cuts for p in cut]
    if not own:
        acc_in, row_in = refs.pop(0), refs.pop(0)
    if last:
        o_refs = (refs.pop(0), refs.pop(0))
    acc_out, row_out = refs

    def tile(which, side, p, c):
        ref, at = kv[side][p]
        return ref[which, at, c]

    def run(which, places, cols):
        wide = len(cols) * BLOCK
        parts = []
        for p, side in places:
            ref, at = kv[side][p]
            parts.append(ref[which, at, cols[0] : cols[-1] + 1].reshape(wide, HEAD_DIM))
        return jnp.concatenate(parts, axis=0)

    worst = jnp.zeros((1, BLOCK), F32)
    for b in range(3):
        if b not in q_bands:
            for c in range(3):
                acc_out[3 * b + c] = acc_in[3 * b + c]
                row_out[3 * b + c] = row_in[3 * b + c]
    accs, totals, tops = {}, {}, {}
    tasks = [(c, bands, keys) for c in range(3) for bands, keys in groups(q_bands, k_bands)]
    if not own:
        for c in range(3):
            for b in q_bands:
                at = 3 * b + c
                accs[b, c], totals[b, c], tops[b, c] = acc_in[at], row_in[at, 0:1], row_in[at, 1:2]

    def first_stage(c, bands, keys):
        cols = list(near(c))
        places = [(p, side) for p in keys for side in range(sides)]
        q = jnp.concatenate([q_ref[0, b, c] for b in bands], axis=0)
        scores = lax.dot_general(run(0, places, cols), q, NT, preferred_element_type=F32)
        for n, b in enumerate(bands):
            if (b, c) not in tops:
                mine = (places.index((keys[0], 0)) * len(cols) + cols.index(c)) * BLOCK
                mine = scores[mine : mine + BLOCK, n * BLOCK : (n + 1) * BLOCK]
                tops[b, c] = jnp.max(mine, axis=0, keepdims=True) * SCORE_SCALE
        return scores

    def second_stage(c, bands, keys, scores):
        cols = list(near(c))
        wide = len(cols) * BLOCK
        places = [(p, side) for p in keys for side in range(sides)]
        top = jnp.concatenate([tops[b, c] for b in bands], axis=1)
        shifts = [top] if own else [top + (1 - flag_ref[side]).astype(F32) * 1e30 for side in range(sides)]
        weights = jnp.concatenate(
            [
                jnp.exp2(scores[n * wide : (n + 1) * wide] * SCORE_SCALE - shifts[side]).astype(BF16)
                for n, (p, side) in enumerate(places)
            ],
            axis=0,
        )
        values = run(1, places, cols)
        values = jnp.concatenate([values.T, jnp.ones((16, values.shape[0]), BF16)], axis=0)
        both = jnp.dot(values, weights, preferred_element_type=F32)
        for n, b in enumerate(bands):
            here = both[:, n * BLOCK : (n + 1) * BLOCK]
            acc, total = here[:HEAD_DIM], here[HEAD_DIM : HEAD_DIM + 1]
            accs[b, c] = accs[b, c] + acc if (b, c) in accs else acc
            totals[b, c] = totals[b, c] + total if (b, c) in totals else total

    scores = first_stage(*tasks[0])
    for n, task in enumerate(tasks):
        ahead = first_stage(*tasks[n + 1]) if n + 1 < len(tasks) else None
        second_stage(*task, scores)
        scores = ahead
    for c in range(3):
        for b in q_bands:
            at = 3 * b + c
            acc_out[at] = accs[b, c]
            row_out[at] = jnp.concatenate([totals[b, c], tops[b, c], jnp.zeros((6, BLOCK), F32)], axis=0)
            worst = jnp.maximum(worst, jnp.where(totals[b, c] < OVER, 0.0, 1.0))

    @pl.when(jnp.max(worst) > 0.0)
    def _():
        for b in q_bands:

            def redo(c, carry, b=b):
                at = 3 * b + c
                q = q_ref[0, b, c]
                if own:
                    acc_out[at] = jnp.zeros((HEAD_DIM, BLOCK), F32)
                    row_out[at, 0:1] = jnp.zeros((1, BLOCK), F32)
                    row_out[at, 1:2] = jnp.full((1, BLOCK), LOWEST, F32)
                else:
                    acc_out[at] = acc_in[at]
                    row_out[at] = row_in[at]
                for side in range(sides):
                    for p in k_bands:
                        if p not in near(b):
                            continue

                        def some(k, carry, side=side, p=p):
                            scores = lax.dot_general(tile(0, side, p, k), q, NT, preferred_element_type=F32)
                            before = row_out[at, 1:2]
                            top = jnp.maximum(before, jnp.max(scores, axis=0, keepdims=True) * SCORE_SCALE)
                            weights = jnp.exp2(scores * SCORE_SCALE - top)
                            fade = jnp.exp2(before - top)
                            acc = lax.dot_general(
                                tile(1, side, p, k), weights.astype(BF16), TN, preferred_element_type=F32
                            )
                            acc_out[at] = acc_out[at] * fade + acc
                            row_out[at, 0:1] = row_out[at, 0:1] * fade + jnp.sum(weights, axis=0, keepdims=True)
                            row_out[at, 1:2] = top
                            return carry

                        low, high = jnp.maximum(c - 1, 0), jnp.minimum(c + 1, 2) + 1
                        if own:
                            lax.fori_loop(low, high, some, 0)
                        else:

                            @pl.when(flag_ref[side] != 0)
                            def _(some=some, low=low, high=high):
                                lax.fori_loop(low, high, some, 0)

                return carry

            lax.fori_loop(0, 3, redo, 0)

    if last:
        for b in range(3):
            tiles = [(acc_out[3 * c + b] * (1.0 / row_out[3 * c + b, 0:1])).T for c in range(3)]
            for half in range(2):
                for f in range(3):
                    for n in range(8):
                        row = 8 * b + n
                        at = half * HALF + f * 64 + n * 8
                        slab = jnp.concatenate([t[at : at + 8] for t in tiles], axis=0)
                        o_refs[half][row // 3, f * 3 + row % 3] = slab.astype(BF16)


ACC = (9, HEAD_DIM, BLOCK)
ROW = (9, 8, BLOCK)


def attend(queries, keys_values, cuts, flags=None, state=None, last=False, us=12):
    own = state is None
    k_bands = [p for cut in cuts for p in cut]
    q_bands = [b for b in range(3) if any(p in near(b) for p in k_bands)]
    operands = [queries] + [a for side in keys_values for a in side]
    in_specs = []
    if not own:
        operands = [flags] + operands + list(state)
        in_specs.append(pl.BlockSpec(memory_space=pltpu.SMEM))
    in_specs += [pl.BlockSpec(memory_space=pltpu.VMEM)] * (len(operands) - len(in_specs))
    state_shapes = [jax.ShapeDtypeStruct(ACC, F32), jax.ShapeDtypeStruct(ROW, F32)]
    if last:
        out_shape = [jax.ShapeDtypeStruct((8,) + CHUNK, BF16)] * 2
        scratch = [pltpu.VMEM(s.shape, F32) for s in state_shapes]
    else:
        out_shape, scratch = state_shapes, []
    return pl.pallas_call(
        functools.partial(attend_kernel, (own, last, cuts, q_bands)),
        in_specs=in_specs,
        out_specs=[pl.BlockSpec(memory_space=pltpu.VMEM)] * len(out_shape),
        out_shape=out_shape,
        scratch_shapes=scratch,
        compiler_params=params(24),
        cost_estimate=cost(us),
        name="attend",
    )(*operands)


PLANE = ("ylo", "core", "z", "yhi")


def plane_groups():
    at = lambda ylo, core, n: (ylo * 2 + core) * 8 + n
    return [[at(ylo, core, n) for ylo in (core, 1 - core) for n in range(8)] for core in (0, 1)]


def exchange(x):
    return lax.all_to_all(x, PLANE, 0, 0, axis_index_groups=plane_groups(), tiled=True)


def swap_cores(x):
    return lax.ppermute(x, "core", [(0, 1), (1, 0)])


def from_tile(x, steps):
    at = lambda tile: (tile % 4) * 2 + tile // 4
    return lax.ppermute(x, ("x", "core"), [(at(t), at(t + steps)) for t in range(8) if 0 <= t + steps < 8])


CUTS = ((0, 1), (2,))


def body(query_band, key_band, value_band):
    core_index = lax.axis_index("core").astype(jnp.int32)
    core = core_index.reshape(1)
    tile = core_index * 4 + lax.axis_index("x").astype(jnp.int32)
    flags = jnp.stack([tile > 0, tile < 7]).astype(jnp.int32)
    got = exchange(pack(core, pack_first_kernel, 16, FIRST, key_band, value_band))
    rest = pack(core, pack_second_kernel, 24, SECOND, key_band, value_band, query_band)
    rest, got = lax.optimization_barrier((rest, got))
    came = swap_cores(got[8:])
    got_rest = exchange(rest)
    (first,) = assemble(assemble_first_kernel, got, came, (2, 2))
    near_first = [from_tile(first, s) for s in (1, -1)]
    came_kv, came_q = (swap_cores(got_rest[8:, :, cut]) for cut in (slice(0, 16), slice(16, 40)))
    (second,) = assemble(assemble_second_kernel, got_rest, came_kv, (2, 1))
    (queries,) = assemble(assemble_queries_kernel, got_rest, came_q, (1, 3))
    second, queries = lax.optimization_barrier((second, queries))
    near_second = [from_tile(second, s) for s in (1, -1)]
    state = attend(queries, [[first, second]], CUTS, us=9)
    state = attend(queries, [[a] for a in near_first], CUTS[:1], flags, state, us=10)
    kept, sent = attend(queries, [[a] for a in near_second], CUTS[1:], flags, state, last=True, us=5)
    back = jnp.concatenate([kept, swap_cores(sent)], axis=0)
    return unpack(core, exchange(back))


def solution(mesh):
    split = Mesh(mesh.devices.reshape(2, 4, 2, 4, 2), ("ylo", "x", "core", "z", "yhi"))
    spec = P(("ylo", "x", "core"), ("z", "yhi"), None, None)
    return jax.shard_map(body, mesh=split, in_specs=(spec, spec, spec), out_specs=spec, check_vma=False)
```

```python
import functools

import jax
import jax.numpy as jnp
from jax import lax
from jax.experimental import pallas as pl
from jax.experimental.pallas import tpu as pltpu
from jax.sharding import Mesh, PartitionSpec as P

HEAD_DIM = 128
HEADS = 16
BLOCK = 384
HALF = 192
SCORE_SCALE = HEAD_DIM ** (-0.5) * 1.4426950408889634
LOWEST = -1e30
OVER = 2.0**100
BF16 = jnp.bfloat16
F32 = jnp.float32
CHUNK = (9, 24, HEAD_DIM)
NT = (((1,), (1,)), ((), ()))
TN = (((0,), (0,)), ((), ()))


def params(mib):
    return pltpu.CompilerParams(vmem_limit_bytes=mib * 1024 * 1024)


def cost(us):
    return pl.CostEstimate(flops=int(us * 1e6), bytes_accessed=int(us * 1e4), transcendentals=0)


def pack_first_kernel(core_ref, *refs):
    o_ref = refs[-1]
    for n, x_ref in enumerate(refs[:-1]):
        for h in range(8):
            o_ref[h, n] = x_ref[:, :, :, h * HEAD_DIM : (h + 1) * HEAD_DIM].reshape(9, 16, HEAD_DIM)


def pack_second_kernel(core_ref, key_ref, value_ref, query_ref, o_ref):
    for h in range(8):
        lanes = slice(h * HEAD_DIM, (h + 1) * HEAD_DIM)
        for n in range(9):
            last = [ref[n // 3, n % 3, 16:24, lanes].astype(F32) for ref in (key_ref, value_ref)]
            o_ref[h, n, 0:16] = jnp.concatenate(last, axis=0).astype(BF16)
            o_ref[h, n, 16:40] = query_ref[n // 3, n % 3, :, lanes]


def pack(core, kernel, columns, inner, *bands):
    return pl.pallas_call(
        kernel,
        grid_spec=pltpu.PrefetchScalarGridSpec(
            num_scalar_prefetch=1,
            grid=(2,),
            in_specs=[pl.BlockSpec((3, 3, columns, 1024), lambda j, s: (0, 0, 0, (j + s[0]) % 2))] * len(bands),
            out_specs=pl.BlockSpec((8,) + inner, lambda j, s: (j,) + (0,) * len(inner)),
        ),
        out_shape=jax.ShapeDtypeStruct((HEADS,) + inner, BF16),
        compiler_params=params(56),
        cost_estimate=cost(1.2 * len(bands)),
        name="pack",
    )(core, *bands)


FIRST = (2, 9, 16, HEAD_DIM)
SECOND = (9, 40, HEAD_DIM)


def unpack_kernel(core_ref, x_ref, o_ref):
    for h in range(8):
        o_ref[:, :, :, h * HEAD_DIM : (h + 1) * HEAD_DIM] = x_ref[h].reshape(3, 3, 24, HEAD_DIM)


def unpack(core, x):
    return pl.pallas_call(
        unpack_kernel,
        grid_spec=pltpu.PrefetchScalarGridSpec(
            num_scalar_prefetch=1,
            grid=(2,),
            in_specs=[pl.BlockSpec((8,) + CHUNK, lambda j, s: (j, 0, 0, 0))],
            out_specs=pl.BlockSpec((3, 3, 24, 1024), lambda j, s: (0, 0, 0, (j + s[0]) % 2)),
        ),
        out_shape=jax.ShapeDtypeStruct((3, 3, 24, HEADS * HEAD_DIM), BF16),
        compiler_params=params(12),
        cost_estimate=cost(1),
        name="unpack",
    )(core, x)


def gather(o_refs, slab):
    for b in range(3):
        for half in range(2):
            slabs = [slab(half, row // 3, f * 3 + row % 3) for f in range(3) for row in range(8 * b, 8 * b + 8)]
            for c, (ref, where) in enumerate(o_refs):
                tokens = jnp.concatenate([s[c * 8 : (c + 1) * 8] for s in slabs], axis=0)
                ref[where + (b, pl.ds(half * HALF, HALF))] = tokens.astype(BF16)


def assemble_first_kernel(kept_ref, came_ref, kv_ref):
    halves = (kept_ref, came_ref)
    for m in range(2):
        places = [(kv_ref, (m, c)) for c in range(2)]
        gather(places, lambda half, chunk, n, m=m: halves[half][chunk, m, n].astype(F32))


def assemble_second_kernel(kept_ref, came_ref, kv_ref):
    halves = (kept_ref, came_ref)
    places = [(kv_ref, (m, 0)) for m in range(2)]
    gather(places, lambda half, chunk, n: halves[half][chunk, n, 0:16].astype(F32))


def assemble_queries_kernel(kept_ref, came_ref, q_ref):
    places = [(q_ref, (0, c)) for c in range(3)]
    slab = lambda half, chunk, n: (came_ref[chunk, n] if half else kept_ref[chunk, n, 16:40]).astype(F32)
    gather(places, slab)


def assemble(kernel, got, came, *leads):
    return pl.pallas_call(
        kernel,
        in_specs=[pl.BlockSpec(memory_space=pltpu.VMEM)] * 2,
        out_specs=[pl.BlockSpec(memory_space=pltpu.VMEM)] * len(leads),
        out_shape=[jax.ShapeDtypeStruct(lead + (3, BLOCK, HEAD_DIM), BF16) for lead in leads],
        compiler_params=params(8),
        cost_estimate=cost(16000) if kernel is assemble_first_kernel else cost(1),
        name="assemble",
    )(got, came)


def near(n):
    return range(max(n - 1, 0), min(n + 1, 2) + 1)


def groups(q_bands, k_bands):
    if k_bands == [0, 1, 2]:
        return [((0, 1), (0, 1)), ((1, 2), (2,)), ((2,), (1,))]
    if k_bands == [0, 1]:
        return [((0, 1), (0, 1)), ((2,), (1,))]
    return [(tuple(q_bands), tuple(k_bands))]


def attend_kernel(plan, *refs):
    own, last, cuts, q_bands = plan
    refs = list(refs)
    sides = 1 if own else 2
    flag_ref = None if own else refs.pop(0)
    q_ref = refs.pop(0)
    kv = [{}, {}]
    for side in range(sides):
        for cut in cuts:
            ref = refs.pop(0)
            for p in cut:
                kv[side][p] = (ref, p - cut[0])
    k_bands = [p for cut in cuts for p in cut]
    if not own:
        acc_in, row_in = refs.pop(0), refs.pop(0)
    if last:
        o_refs = (refs.pop(0), refs.pop(0))
    acc_out, row_out = refs

    def tile(which, side, p, c):
        ref, at = kv[side][p]
        return ref[which, at, c]

    def run(which, places, cols):
        wide = len(cols) * BLOCK
        parts = []
        for p, side in places:
            ref, at = kv[side][p]
            parts.append(ref[which, at, cols[0] : cols[-1] + 1].reshape(wide, HEAD_DIM))
        return jnp.concatenate(parts, axis=0)

    worst = jnp.zeros((1, BLOCK), F32)
    for b in range(3):
        if b not in q_bands:
            for c in range(3):
                acc_out[3 * b + c] = acc_in[3 * b + c]
                row_out[3 * b + c] = row_in[3 * b + c]
    accs, totals, tops = {}, {}, {}
    tasks = [(c, bands, keys) for c in range(3) for bands, keys in groups(q_bands, k_bands)]
    if not own:
        for c in range(3):
            for b in q_bands:
                at = 3 * b + c
                accs[b, c], totals[b, c], tops[b, c] = acc_in[at], row_in[at, 0:1], row_in[at, 1:2]

    def first_stage(c, bands, keys):
        cols = list(near(c))
        places = [(p, side) for p in keys for side in range(sides)]
        q = jnp.concatenate([q_ref[0, b, c] for b in bands], axis=0)
        scores = lax.dot_general(run(0, places, cols), q, NT, preferred_element_type=F32)
        for n, b in enumerate(bands):
            if (b, c) not in tops:
                mine = (places.index((b, 0)) * len(cols) + cols.index(c)) * BLOCK
                mine = scores[mine : mine + BLOCK, n * BLOCK : (n + 1) * BLOCK]
                tops[b, c] = jnp.max(mine, axis=0, keepdims=True) * SCORE_SCALE
        return scores

    def second_stage(c, bands, keys, scores):
        cols = list(near(c))
        wide = len(cols) * BLOCK
        places = [(p, side) for p in keys for side in range(sides)]
        top = jnp.concatenate([tops[b, c] for b in bands], axis=1)
        shifts = [top] if own else [top + (1 - flag_ref[side]).astype(F32) * 1e30 for side in range(sides)]
        weights = jnp.concatenate(
            [
                jnp.exp2(scores[n * wide : (n + 1) * wide] * SCORE_SCALE - shifts[side]).astype(BF16)
                for n, (p, side) in enumerate(places)
            ],
            axis=0,
        )
        values = run(1, places, cols)
        values = jnp.concatenate([values.T, jnp.ones((16, values.shape[0]), BF16)], axis=0)
        both = jnp.dot(values, weights, preferred_element_type=F32)
        for n, b in enumerate(bands):
            here = both[:, n * BLOCK : (n + 1) * BLOCK]
            acc, total = here[:HEAD_DIM], here[HEAD_DIM : HEAD_DIM + 1]
            accs[b, c] = accs[b, c] + acc if (b, c) in accs else acc
            totals[b, c] = totals[b, c] + total if (b, c) in totals else total

    scores = first_stage(*tasks[0])
    for n, task in enumerate(tasks):
        ahead = first_stage(*tasks[n + 1]) if n + 1 < len(tasks) else None
        second_stage(*task, scores)
        scores = ahead
    for c in range(3):
        for b in q_bands:
            at = 3 * b + c
            acc_out[at] = accs[b, c]
            row_out[at] = jnp.concatenate([totals[b, c], tops[b, c], jnp.zeros((6, BLOCK), F32)], axis=0)
            worst = jnp.maximum(worst, jnp.where(totals[b, c] < OVER, 0.0, 1.0))

    @pl.when(jnp.max(worst) > 0.0)
    def _():
        for b in q_bands:

            def redo(c, carry, b=b):
                at = 3 * b + c
                q = q_ref[0, b, c]
                if own:
                    acc_out[at] = jnp.zeros((HEAD_DIM, BLOCK), F32)
                    row_out[at, 0:1] = jnp.zeros((1, BLOCK), F32)
                    row_out[at, 1:2] = jnp.full((1, BLOCK), LOWEST, F32)
                else:
                    acc_out[at] = acc_in[at]
                    row_out[at] = row_in[at]
                for side in range(sides):
                    for p in k_bands:
                        if p not in near(b):
                            continue

                        def some(k, carry, side=side, p=p):
                            scores = lax.dot_general(tile(0, side, p, k), q, NT, preferred_element_type=F32)
                            before = row_out[at, 1:2]
                            top = jnp.maximum(before, jnp.max(scores, axis=0, keepdims=True) * SCORE_SCALE)
                            weights = jnp.exp2(scores * SCORE_SCALE - top)
                            fade = jnp.exp2(before - top)
                            acc = lax.dot_general(
                                tile(1, side, p, k), weights.astype(BF16), TN, preferred_element_type=F32
                            )
                            acc_out[at] = acc_out[at] * fade + acc
                            row_out[at, 0:1] = row_out[at, 0:1] * fade + jnp.sum(weights, axis=0, keepdims=True)
                            row_out[at, 1:2] = top
                            return carry

                        low, high = jnp.maximum(c - 1, 0), jnp.minimum(c + 1, 2) + 1
                        if own:
                            lax.fori_loop(low, high, some, 0)
                        else:

                            @pl.when(flag_ref[side] != 0)
                            def _(some=some, low=low, high=high):
                                lax.fori_loop(low, high, some, 0)

                return carry

            lax.fori_loop(0, 3, redo, 0)

    if last:
        for b in range(3):
            tiles = [(acc_out[3 * c + b] * (1.0 / row_out[3 * c + b, 0:1])).T for c in range(3)]
            for half in range(2):
                for f in range(3):
                    for n in range(8):
                        row = 8 * b + n
                        at = half * HALF + f * 64 + n * 8
                        slab = jnp.concatenate([t[at : at + 8] for t in tiles], axis=0)
                        o_refs[half][row // 3, f * 3 + row % 3] = slab.astype(BF16)


ACC = (9, HEAD_DIM, BLOCK)
ROW = (9, 8, BLOCK)


def attend(queries, keys_values, cuts, flags=None, state=None, last=False, us=12):
    own = state is None
    k_bands = [p for cut in cuts for p in cut]
    q_bands = [b for b in range(3) if any(p in near(b) for p in k_bands)]
    operands = [queries] + [a for side in keys_values for a in side]
    in_specs = []
    if not own:
        operands = [flags] + operands + list(state)
        in_specs.append(pl.BlockSpec(memory_space=pltpu.SMEM))
    in_specs += [pl.BlockSpec(memory_space=pltpu.VMEM)] * (len(operands) - len(in_specs))
    state_shapes = [jax.ShapeDtypeStruct(ACC, F32), jax.ShapeDtypeStruct(ROW, F32)]
    if last:
        out_shape = [jax.ShapeDtypeStruct((8,) + CHUNK, BF16)] * 2
        scratch = [pltpu.VMEM(s.shape, F32) for s in state_shapes]
    else:
        out_shape, scratch = state_shapes, []
    return pl.pallas_call(
        functools.partial(attend_kernel, (own, last, cuts, q_bands)),
        in_specs=in_specs,
        out_specs=[pl.BlockSpec(memory_space=pltpu.VMEM)] * len(out_shape),
        out_shape=out_shape,
        scratch_shapes=scratch,
        compiler_params=params(24),
        cost_estimate=cost(us),
        name="attend",
    )(*operands)


PLANE = ("ylo", "core", "z", "yhi")


def plane_groups():
    at = lambda ylo, core, n: (ylo * 2 + core) * 8 + n
    return [[at(ylo, core, n) for ylo in (core, 1 - core) for n in range(8)] for core in (0, 1)]


def exchange(x):
    return lax.all_to_all(x, PLANE, 0, 0, axis_index_groups=plane_groups(), tiled=True)


def swap_cores(x):
    return lax.ppermute(x, "core", [(0, 1), (1, 0)])


def from_tile(x, steps):
    at = lambda tile: (tile % 4) * 2 + tile // 4
    return lax.ppermute(x, ("x", "core"), [(at(t), at(t + steps)) for t in range(8) if 0 <= t + steps < 8])


CUTS = ((0, 1), (2,))


def body(query_band, key_band, value_band):
    core_index = lax.axis_index("core").astype(jnp.int32)
    core = core_index.reshape(1)
    tile = core_index * 4 + lax.axis_index("x").astype(jnp.int32)
    flags = jnp.stack([tile > 0, tile < 7]).astype(jnp.int32)
    got = exchange(pack(core, pack_first_kernel, 16, FIRST, key_band, value_band))
    rest = pack(core, pack_second_kernel, 24, SECOND, key_band, value_band, query_band)
    rest, got = lax.optimization_barrier((rest, got))
    came = swap_cores(got[8:])
    got_rest = exchange(rest)
    (first,) = assemble(assemble_first_kernel, got, came, (2, 2))
    near_first = [from_tile(first, s) for s in (1, -1)]
    came_kv, came_q = (swap_cores(got_rest[8:, :, cut]) for cut in (slice(0, 16), slice(16, 40)))
    (second,) = assemble(assemble_second_kernel, got_rest, came_kv, (2, 1))
    (queries,) = assemble(assemble_queries_kernel, got_rest, came_q, (1, 3))
    second, queries = lax.optimization_barrier((second, queries))
    near_second = [from_tile(second, s) for s in (1, -1)]
    state = attend(queries, [[first, second]], CUTS, us=9)
    state = attend(queries, [[a] for a in near_first], CUTS[:1], flags, state, us=10)
    kept, sent = attend(queries, [[a] for a in near_second], CUTS[1:], flags, state, last=True, us=5)
    back = jnp.concatenate([kept, swap_cores(sent)], axis=0)
    return unpack(core, exchange(back))


def solution(mesh):
    split = Mesh(mesh.devices.reshape(2, 4, 2, 4, 2), ("ylo", "x", "core", "z", "yhi"))
    spec = P(("ylo", "x", "core"), ("z", "yhi"), None, None)
    return jax.shard_map(body, mesh=split, in_specs=(spec, spec, spec), out_specs=spec, check_vma=False)
```
